512 devices in a mesh: bins: 4 (over y), ctx: 128 (over x, z, core).
Axes of the slice: x: 4, y: 4, z: 16, core: 2. Of those that a mesh axis runs over, the one named last changes fastest.
Arguments:
- hyena_input: bfloat16 [4, 16384, 2048], P('bins', 'ctx'), may hold values from -6 to 6
- hyena_gate: bfloat16 [4, 16384, 2048], P('bins', 'ctx'), may hold values from -6 to 6
- residues: float32 [16, 2048], replicated, may hold values from -0.2581989 to 0.2581989
- decay_rates: float32 [16, 2048], replicated, may hold values from 6.1035156e-06 to 0.0333333333
- skip_weight: float32 [2048], replicated, may hold values from 0.5 to 1.5
- queries: bfloat16 [4, 16384, 2048], P('bins', 'ctx'), may hold values from -4.5 to 4.5
- keys: bfloat16 [4, 16384, 2048], P('bins', 'ctx'), may hold values from -4.5 to 4.5
- document_ids: int32 [4, 16384], P('bins', 'ctx'), may hold values from 0 to 255, never falling along the last dimension, each value on 1 to 128 neighbouring positions
- block_source: int32 [4, 256], P('bins', 'ctx'), may hold values from 0 to 7, as said below
Outputs:
- repacked: bfloat16 [4, 16384, 2048], P('bins', 'ctx')
The draws below stay inside these ranges and needn't reach their ends.
Inputs may be any that keep to these rules, and one draw needn't show every extreme that they name: `document_ids`: ids never fall along a bin; every document holds 1 to 128 positions, and one holds exactly 128. `block_source`: A given permutation for each device column: for blocks j with the same j // 2, the 8 entries of all bins are all different.
All inputs are finite; a program needn't handle non-finite values.
Results may differ from the reference program's by a relative error of at most 0.0056.
Values may be sent and summed in bfloat16 or wider, within the bound.
A program may use at most 128 MiB of HBM per device.

```python
import math
import jax
import jax.numpy as jnp
import numpy as np
from jax import lax

CHANNELS = 2048
HEADS = 16
HEAD_DIM = 128
MODES = 16
TOK_DEV = 128
BLOCK = 64
BINS = 4
LENGTH = 16384
BLK_DEV = 2
BLOCKS = 256
DOCS = 256


def mode_rates(key, slow_share):
    key = jax.random.fold_in(key, 101)
    key_one, key_two, key_three = jax.random.split(key, 3)
    slow_rates = jnp.exp(jax.random.uniform(key_one, (MODES, CHANNELS), jnp.float32, math.log(0.1), math.log(2.3))) / LENGTH
    fast_rates = jnp.exp(jax.random.uniform(key_two, (MODES, CHANNELS), jnp.float32, math.log(1.0 / 50.0), math.log(1.0 / 30.0)))
    chosen = jax.random.uniform(key_three, (MODES, CHANNELS), jnp.float32) < slow_share
    return jnp.where(chosen, slow_rates, fast_rates)


def draw_decay_rates(key, part):
    return mode_rates(key, 0.5)


def draw_residues(key, part):
    decay_values = mode_rates(key, 0.5)
    key = jax.random.fold_in(key, 7)
    samples = jnp.clip(jax.random.normal(key, (MODES, CHANNELS), jnp.float32), -4.0, 4.0)
    return samples * jnp.sqrt(2.0 * decay_values / MODES)


def draw_queries(key, part):
    key = jax.random.fold_in(key, 31)
    return jnp.clip(jax.random.normal(key, (BINS, LENGTH, CHANNELS), jnp.float32), -4.0, 4.0).astype(jnp.bfloat16)


def draw_keys(key, part):
    key = jax.random.fold_in(key, 37)
    return jnp.clip(jax.random.normal(key, (BINS, LENGTH, CHANNELS), jnp.float32), -4.0, 4.0).astype(jnp.bfloat16)


def draw_block_source(key, part):
    key = jax.random.fold_in(key, 5)
    column_count = BLOCKS // BLK_DEV
    column_keys = jax.random.split(key, column_count)
    orders = jax.vmap(lambda column_key: jax.random.permutation(column_key, BINS * BLK_DEV))(column_keys)
    arranged = orders.reshape(column_count, BINS, BLK_DEV).transpose(1, 0, 2)
    return arranged.reshape(BINS, BLOCKS).astype(jnp.int32)


def block_scale(rng, dims, cuts, least, top_value):
    loudness = 1.0
    for position, shards_of in cuts:
        heights = jax.random.uniform(jax.random.fold_in(jax.random.fold_in(rng, 6), position), (shards_of,), jnp.float32, least / len(cuts), top_value / len(cuts))
        loudness = loudness * jnp.repeat(jnp.exp(heights), dims[position] // shards_of).reshape((-1,) + (1,) * (len(dims) - 1 - position))
    return loudness


def profile(count, total, most, skew):
    weights = [(1 << 20) // math.isqrt(standing ** skew) + 1 for standing in range(2, count + 1)]
    surplus, given = total - most - (count - 1), [1] * (count - 1)
    while surplus > 0:
        movable = [i for i in range(count - 1) if given[i] < most]
        pool, budget = sum([weights[i] for i in movable]), surplus
        for i in movable:
            addition = min(most - given[i], max(1, budget * weights[i] // pool), surplus)
            given[i] = given[i] + addition
            surplus = surplus - addition
    return np.array([most] + given)


def ragged(own_key, amount, total, reach, slope):
    if amount == 2:
        one = jax.random.randint(own_key, (), max(1, total - reach), min(reach, total - 1) + 1)
        return jnp.stack([one, total - one])
    tallies = jnp.asarray(profile(amount, total, reach, slope), jnp.int32)
    couples = (amount - 1) // 2
    donor, receiver = tallies[1:1 + 2 * couples:2], tallies[2:2 + 2 * couples:2]
    margin = jnp.minimum(donor - 1, reach - receiver)
    moved = jax.random.randint(jax.random.fold_in(own_key, 1), (couples,), 0, 1 << 20) % (margin + 1)
    tallies = tallies.at[1:1 + 2 * couples:2].set(donor - moved).at[2:2 + 2 * couples:2].set(receiver + moved)
    return tallies[jax.random.permutation(jax.random.fold_in(own_key, 2), amount)]


def centred(own_key, dims, scale, bound, cuts=(), dtype=jnp.bfloat16):
    values = jax.random.normal(own_key, dims, jnp.float32) * scale
    if len(cuts) > 0:
        values = block_scale(own_key, dims, cuts, -0.22, 0.18) * values
    return jnp.clip(values, min=-bound, max=bound).astype(dtype)


def setup_inputs(seed: int = 0) -> dict:
    arg_keys = jax.random.split(jax.random.key(seed), 10)
    return {
        "hyena_input": centred(arg_keys[0], (BINS, LENGTH, CHANNELS), 1.0, 6.0, ((0, 4), (1, 128))),
        "hyena_gate": centred(arg_keys[1], (BINS, LENGTH, CHANNELS), 1.0, 6.0, ((0, 4), (1, 128))),
        "residues": draw_residues(jax.random.fold_in(arg_keys[9], 71), 0),
        "decay_rates": draw_decay_rates(jax.random.fold_in(arg_keys[9], 71), 0),
        "skip_weight": jnp.clip(jax.random.uniform(arg_keys[4], (CHANNELS,), jnp.float32, 0.5, 1.5), 0.5, 1.5),
        "queries": draw_queries(jax.random.fold_in(arg_keys[9], 71), 0),
        "keys": draw_keys(jax.random.fold_in(arg_keys[9], 71), 0),
        "document_ids": jax.vmap(lambda own: jnp.searchsorted(jnp.cumsum(ragged(own, DOCS, LENGTH, TOK_DEV, 2)), jnp.arange(LENGTH), side="right"))(jax.random.split(arg_keys[7], BINS)).reshape((BINS, LENGTH)).astype(jnp.int32),
        "block_source": draw_block_source(jax.random.fold_in(arg_keys[9], 71), 0),
    }


def long_filter(weight_part, decay_part, length_total):
    lag_values = jnp.arange(length_total).astype(jnp.float32)[:, None]
    total_sum = jnp.zeros((length_total, weight_part.shape[1]), jnp.float32)
    for mode_index in range(weight_part.shape[0]):
        total_sum = total_sum + weight_part[mode_index][None, :] * jnp.exp(-decay_part[mode_index][None, :] * lag_values)
    return total_sum


def long_convolution(signal, residues, decay_rates):
    length_total, channel_count = signal.shape
    group_count = channel_count // 128
    signal_groups = signal.reshape(length_total, group_count, 128).transpose(1, 0, 2)
    weight_groups = residues.reshape(MODES, group_count, 128).transpose(1, 0, 2)
    decay_groups = decay_rates.reshape(MODES, group_count, 128).transpose(1, 0, 2)

    def one_group(operands):
        group_signal, group_weight, group_decay = operands
        kernel = long_filter(group_weight, group_decay, length_total)
        padded_len = 2 * length_total
        spectrum = jnp.fft.rfft(group_signal, padded_len, axis=0) * jnp.fft.rfft(kernel, padded_len, axis=0)
        return jnp.fft.irfft(spectrum, padded_len, axis=0)[:length_total].astype(jnp.float32)

    result = lax.map(one_group, (signal_groups, weight_groups, decay_groups))
    return result.transpose(1, 0, 2).reshape(length_total, channel_count)


def attend(query_rows, query_ids, query_pos, key_rows, value_rows, key_ids, key_pos):
    row_count = query_rows.shape[0]
    span_count = key_rows.shape[0]
    query_heads = query_rows.reshape(row_count, HEADS, HEAD_DIM).astype(jnp.float32)
    key_heads = key_rows.reshape(span_count, HEADS, HEAD_DIM).astype(jnp.float32)
    scores = jnp.einsum("bhd,whd->hbw", query_heads, key_heads) * (HEAD_DIM ** -0.5)
    allowed = (query_ids[:, None] == key_ids[None, :]) & (key_pos[None, :] <= query_pos[:, None])
    scores = jnp.where(allowed[None], scores, -1e30)
    row_max = jnp.max(scores, axis=2, keepdims=True)
    weights = jnp.exp(scores - row_max)
    weights = (weights / jnp.sum(weights, axis=2, keepdims=True)).astype(jnp.bfloat16)
    value_heads = value_rows.reshape(span_count, HEADS, HEAD_DIM).astype(jnp.float32)
    mixed = jnp.einsum("hbw,whd->bhd", weights.astype(jnp.float32), value_heads)
    return mixed.reshape(row_count, HEADS * HEAD_DIM).astype(jnp.bfloat16)


def bin_attention(query_bin, key_bin, value_bin, id_bin):
    key_padded = jnp.concatenate([jnp.zeros((TOK_DEV, CHANNELS), jnp.bfloat16), key_bin], axis=0)
    value_padded = jnp.concatenate([jnp.zeros((TOK_DEV, CHANNELS), jnp.bfloat16), value_bin], axis=0)
    shifted_ids = (id_bin + 1).astype(jnp.int32)
    id_padded = jnp.concatenate([jnp.zeros((TOK_DEV,), jnp.int32), shifted_ids], axis=0)
    query_pos = (jnp.arange(BLOCK) + TOK_DEV).astype(jnp.int32)
    key_pos = jnp.arange(TOK_DEV + BLOCK).astype(jnp.int32)

    def one_block(block_index):
        start_row = (block_index * BLOCK).astype(jnp.int32)
        query_part = lax.dynamic_slice_in_dim(query_bin, start_row, BLOCK, 0)
        query_idpart = lax.dynamic_slice_in_dim(shifted_ids, start_row, BLOCK, 0)
        key_part = lax.dynamic_slice_in_dim(key_padded, start_row, TOK_DEV + BLOCK, 0)
        value_part = lax.dynamic_slice_in_dim(value_padded, start_row, TOK_DEV + BLOCK, 0)
        key_idpart = lax.dynamic_slice_in_dim(id_padded, start_row, TOK_DEV + BLOCK, 0)
        return attend(query_part, query_idpart, query_pos, key_part, value_part, key_idpart, key_pos)

    return lax.map(one_block, jnp.arange(BLOCKS).astype(jnp.int32))


def reference(hyena_input, hyena_gate, residues, decay_rates, skip_weight, queries, keys, document_ids, block_source):
    attended_bins = []
    for bin_index in range(BINS):
        signal = hyena_input[bin_index].astype(jnp.float32)
        convolved = long_convolution(signal, residues, decay_rates)
        gate_rows = hyena_gate[bin_index].astype(jnp.float32)
        values = (gate_rows * (convolved + skip_weight[None, :] * signal)).astype(jnp.bfloat16)
        attended_bins.append(bin_attention(queries[bin_index], keys[bin_index], values, document_ids[bin_index]))
    attended = jnp.stack(attended_bins, axis=0)
    columns = (jnp.arange(BLOCKS) // BLK_DEV).astype(jnp.int32)
    source_bin = block_source // BLK_DEV
    source_block = columns[None, :] * BLK_DEV + block_source % BLK_DEV
    picked = attended[source_bin, source_block]
    return picked.reshape(BINS, LENGTH, CHANNELS)
```

```python
import functools

import jax
import jax.numpy as jnp
from jax import lax
from jax.experimental import pallas as pl
from jax.experimental.pallas import tpu as pltpu
from jax.sharding import PartitionSpec as P

MESH = pl.DeviceIdType.MESH
HEAD_DIM = 128
SUB = 8
F32 = jnp.float32
BF16 = jnp.bfloat16
STATE = BF16


def plan(mesh_shape):
    bins, ctx = mesh_shape["bins"], mesh_shape["ctx"]
    near = 8 if ctx >= 64 else 2
    groups = ctx // near
    far_z = 4 if groups >= 16 else 2
    return bins, ctx, near, groups, far_z, groups // far_z


def kernel(
    dims,
    x_h, g_h, res_h, lam_h, skip_h, q_h, k_h, ids_h, bs_s,
    out_h,
    x_v, g_v, res_v, lam_v, skip_v, q_v, k_v, ids_v,
    xf, xs, pm, ta, ta16, ta32, ta64, et, e_s, e_r, pre, t_s, t_r, c_s, c_r,
    w_v, p_v, w_t, g_t, p_t, k_n, id_s, id_n, bs_own, bs_t, bias, low, upp,
    gtab, ta8, ct, v_s, v_n, o_f, o_s,
    loc, l1s, l1r, l2s, l2r, l3s, l3r, gs, gr, ws, wr, ps, pr, bss, bsr,
    ks, kr, ids_, idr, vs, vr, os_, or_, oloc, sem2, sem3,
):
    bins, ctx, near, groups, far_z, far_x, tokens, channels, modes = dims
    lane_groups = channels // 128
    own = lane_groups // near
    hg = lane_groups // bins
    width = hg * 128
    parts = hg // own
    chunk = tokens // SUB
    half = tokens // 2

    b = lax.axis_index("bins")
    c = lax.axis_index("ctx")
    grp = c // near
    q = c % near
    gx, gz = grp // far_z, grp % far_z
    home = (q * own) // hg
    nxt = (c + 1) % ctx
    prv = (c + ctx - 1) % ctx

    def remote(src, dst, ss, rs, dev):
        return pltpu.make_async_remote_copy(
            src_ref=src, dst_ref=dst, send_sem=ss, recv_sem=rs, device_id=dev, device_id_type=MESH
        )

    def lanes(index):
        return pl.ds(pl.multiple_of(index * 128, 128), 128)

    def cols(index):
        return pl.ds(pl.multiple_of(index * width, 128), width)

    loads = []
    for n, (s, d) in enumerate(
        [(x_h.at[0], x_v), (lam_h, lam_v), (res_h, res_v), (skip_h, skip_v), (g_h.at[0], g_v),
         (k_h.at[0], k_v), (q_h.at[0], q_v), (ids_h, ids_v)]
    ):
        load = pltpu.make_async_copy(s, d, loc.at[n])
        load.start()
        loads.append(load)

    bar = pltpu.get_barrier_semaphore()

    def greet(dev):
        pl.semaphore_signal(bar, inc=1, device_id=dev, device_id_type=MESH)

    count = 0
    for k in range(1, near):
        greet((b, grp * near + (q + k) % near))
        count += 1
    for k in range(1, bins):
        greet(((b + k) % bins, c))
        count += 1
    greet((b, prv))
    count += 1
    mine = [[(bb, grp * near + b * parts + r) for r in range(parts)] for bb in range(bins)]
    for bb in range(bins):
        for r in range(parts):
            same = (bb == b) & (b * parts + r == q)

            @pl.when(jnp.logical_not(same))
            def _():
                greet(mine[bb][r])

    targets = [(home, grp * near + (q + k) % near) for k in range(near)]
    count = count + near - jnp.where(home == b, 1, 0)
    hops = [(b, ((gx + k) % far_x) * far_z * near + gz * near + q) for k in range(1, far_x)]
    zhops = [(b, (gx * far_z + (gz + k) % far_z) * near + q) for k in (1, far_z - 1)]
    for dev in hops + zhops:
        greet(dev)
    count = count + len(hops) + len(zhops)

    loads[0].wait()
    loads[1].wait()
    row = lax.broadcasted_iota(jnp.int32, (SUB, 128), 0)
    m1 = (row >= 1).astype(F32)
    m2 = (row >= 2).astype(F32)
    m4 = (row >= 4).astype(F32)

    def wide(ref, g, m):
        return jnp.broadcast_to(ref[g, pl.ds(m, 1), :], (SUB, 128))

    def states(g):
        rate = lam_v[:, lanes(g)]
        ta[g] = jnp.exp(-rate)
        ta16[g] = jnp.exp(rate * (-1.0 * chunk))
        ta32[g] = jnp.exp(rate * (-2.0 * chunk))
        ta64[g] = jnp.exp(rate * (-4.0 * chunk))
        xf[...] = x_v[:, lanes(g)].astype(F32)
        xt = [xf[pl.ds(t, SUB, stride=chunk), :] for t in range(chunk)]
        for t in range(chunk):
            xs[g, t] = xt[t]
        for m in range(modes):
            a = wide(ta, g, m)
            e = xt[0]
            for t in range(1, chunk):
                e = e * a + xt[t]
            e = e + (wide(ta16, g, m) * m1) * pltpu.roll(e, 1, 0)
            e = e + (wide(ta32, g, m) * m2) * pltpu.roll(e, 2, 0)
            e = e + (wide(ta64, g, m) * m4) * pltpu.roll(e, 4, 0)
            pm[g, m] = pltpu.roll(e, 1, 0) * m1
            et[pl.ds(m, 1), :] = e[SUB - 1 :, :]
        e_s[g] = et[...].astype(STATE)

    def to_near(peer):
        return remote(
            e_s.at[pl.ds(peer * own, own)], e_r.at[q], l1s.at[peer], l1r.at[q], (b, grp * near + peer)
        )

    def state_step(k, carry):
        peer = (q + 1 + k) % near
        for j in range(own):
            states(peer * own + j)
        return carry

    def state_send_step(k, carry):
        carry = state_step(k, carry)
        peer = (q + 1 + k) % near

        @pl.when(peer != q)
        def _():
            to_near(peer).start()

        return carry

    lax.fori_loop(0, near // 2, state_step, 0)
    pl.semaphore_wait(bar, count)
    for k in range(near // 2):
        to_near((q + 1 + k) % near).start()
    loads[4].wait()
    for k in range(1, bins):
        to = (b + k) % bins
        remote(g_v.at[:, cols(to)], g_t.at[b], gs.at[to], gr.at[b], (to, c)).start()
    for dev in hops + zhops:
        pl.semaphore_signal(sem2, inc=1, device_id=dev, device_id_type=MESH)
    lax.fori_loop(near // 2, near, state_send_step, 0)
    e_r[q] = e_s[pl.ds(q * own, own)]

    for n in (2, 3, 5, 6, 7):
        loads[n].wait()
    key_send = remote(k_v, k_n, ks, kr, (b, nxt))
    key_send.start()
    id_s[...] = jnp.broadcast_to(ids_v[...], (SUB, 128))
    id_send = remote(id_s, id_n, ids_, idr, (b, nxt))
    id_send.start()
    block_row = jnp.where(row == 0, bs_s[0, 0], bs_s[0, 1])
    bs_own[...] = block_row
    bs_t[b] = block_row
    for k in range(1, bins):
        to = (b + k) % bins
        remote(bs_own, bs_t.at[b], bss.at[to], bsr.at[b], (to, c)).start()
    own_gate = pltpu.make_async_copy(g_v.at[:, cols(b)], g_t.at[b], oloc.at[0])
    own_gate.start()

    def values_here(g):
        xt = [xs[g, t] for t in range(chunk)]
        cur = res_v[:, lanes(g)]
        rate = ta[g]
        taps = []
        for t in range(chunk):
            taps.append(jnp.broadcast_to(jnp.sum(cur, axis=0, keepdims=True), (SUB, 128)))
            cur = cur * rate
            if t == 0:
                et[...] = cur
        skip = jnp.broadcast_to(skip_v[:, lanes(g)], (SUB, 128))
        y = []
        for t in range(chunk):
            acc = (skip + taps[0]) * xt[t]
            for k in range(1, t + 1):
                acc = acc + taps[k] * xt[t - k]
            y.append(acc)
        for m in range(modes):
            a = wide(ta, g, m)
            d = jnp.broadcast_to(et[pl.ds(m, 1), :], (SUB, 128)) * pm[g, m]
            for t in range(chunk):
                y[t] = y[t] + d
                if t + 1 < chunk:
                    d = d * a
        for t in range(chunk):
            xf[pl.ds(t, SUB, stride=chunk), :] = y[t]
        w_v[:, lanes(g)] = (g_v[:, lanes(g)].astype(F32) * xf[...]).astype(BF16)

    def values_step(n, carry):
        to = (b + 1 + n) % bins

        def one(j, inner):
            values_here(to * hg + j)
            return inner

        lax.fori_loop(0, hg, one, 0)

        @pl.when(to != b)
        def _():
            remote(w_v.at[:, cols(to)], w_t.at[b], ws.at[to], wr.at[b], (to, c)).start()

        return carry

    lax.fori_loop(0, bins // 2, values_step, 0)

    pl.semaphore_wait(sem2, len(hops) + len(zhops))
    for dev in zhops:
        pl.semaphore_signal(sem3, inc=1, device_id=dev, device_id_type=MESH)
    for k in range(1, near):
        peer = (q + k) % near
        remote(e_s.at[pl.ds(0, own)], e_r.at[peer], l1s.at[peer], l1r.at[peer], (b, c)).wait_recv()
    step, leap = [], []
    for j in range(own):
        rate = lam_v[:, lanes(q * own + j)]
        step.append(jnp.exp(rate * (-1.0 * tokens)))
        leap.append(jnp.exp(rate * (-1.0 * tokens * near)))
        acc = jnp.zeros((modes, 128), F32)
        for n in range(near):
            pre[n, j] = acc
            acc = step[j] * acc + e_r[n, j].astype(F32)
        t_s[j] = acc.astype(STATE)
    pl.semaphore_wait(sem3, 2)

    def to_later(k):
        return remote(t_s, t_r.at[grp], l2s.at[k], l2r.at[grp], (b, (grp + k) * near + q))

    for k in range(1, groups):

        @pl.when(grp + k < groups)
        def _():
            to_later(k).start()

    lax.fori_loop(bins // 2, bins, values_step, 0)
    own_part = pltpu.make_async_copy(w_v.at[:, cols(b)], w_t.at[b], oloc.at[1])
    own_part.start()

    key_send.wait_recv()
    id_send.wait_recv()
    t_idx = lax.broadcasted_iota(jnp.int32, (tokens, tokens), 0)
    u_idx = lax.broadcasted_iota(jnp.int32, (tokens, tokens), 1)
    lower = u_idx <= t_idx
    low[...] = lower.astype(F32).astype(BF16)
    upp[...] = (u_idx > t_idx).astype(F32).astype(BF16)
    id_row = jnp.broadcast_to(id_s[0:1, :].astype(F32), (tokens, tokens))
    id_col = id_row.T
    shut = jnp.where(c == 0, 65536.0, 0.0)
    id_before = jnp.broadcast_to(id_n[0:1, :].astype(F32), (tokens, tokens)) + shut
    id_key = jnp.where(lower, id_row, id_before)
    bias[...] = jnp.where(id_key == id_col, 0.0, -1e30)

    def weights_step(n, carry):
        to = (b + 1 + n) % bins
        for j in range(hg):
            h = to * hg + j
            query = q_v[:, lanes(h)]
            dn = (((1,), (1,)), ((), ()))
            s_own = lax.dot_general(query, k_v[:, lanes(h)], dn, preferred_element_type=F32)
            s_prev = lax.dot_general(query, k_n[:, lanes(h)], dn, preferred_element_type=F32)
            u_i = lax.broadcasted_iota(jnp.int32, (tokens, tokens), 1)
            t_i = lax.broadcasted_iota(jnp.int32, (tokens, tokens), 0)
            s = jnp.where(u_i <= t_i, s_own, s_prev) * HEAD_DIM ** (-0.5) + bias[...]
            e = jnp.exp(s - jnp.max(s, axis=1, keepdims=True))
            p_v[h] = (e * (1.0 / jnp.sum(e, axis=1, keepdims=True))).astype(BF16)

        @pl.when(to != b)
        def _():
            remote(p_v.at[pl.ds(to * hg, hg)], p_t.at[b], ps.at[to], pr.at[b], (to, c)).start()

        return carry

    lax.fori_loop(0, bins, weights_step, 0)
    own_weights = pltpu.make_async_copy(p_v.at[pl.ds(b * hg, hg)], p_t.at[b], oloc.at[2])
    own_weights.start()

    ramp = (row + 1).astype(F32)

    def table_step(j, carry):
        g = b * hg + j
        ta8[j] = jnp.exp(lam_v[:, lanes(g)] * (-1.0 * SUB))
        for m in range(modes):
            rate = jnp.broadcast_to(lam_v[pl.ds(m, 1), lanes(g)], (SUB, 128))
            weight = jnp.broadcast_to(res_v[pl.ds(m, 1), lanes(g)], (SUB, 128))
            gtab[j, m] = weight * jnp.exp(-rate * ramp)
        return carry

    lax.fori_loop(0, hg, table_step, 0)

    def earlier(n, carry):
        remote(t_s, t_r.at[n], l2s.at[0], l2r.at[n], (b, c)).wait_recv()
        return tuple(leap[j] * carry[j] + t_r[n, j].astype(F32) for j in range(own))

    start = lax.fori_loop(0, grp, earlier, tuple(jnp.zeros((modes, 128), F32) for _ in range(own)))
    for j in range(own):
        power = start[j]
        for n in range(near):
            c_s[n, j] = (pre[n, j] + power).astype(STATE)
            power = power * step[j]
    spot = pl.ds((q % parts) * own, own)

    def to_home(k):
        n = (q + k) % near
        return remote(c_s.at[n], c_r.at[b, spot], l3s.at[k], l3r.at[b, q % parts], targets[k])

    for k in range(1, near):
        to_home(k).start()

    @pl.when(home != b)
    def _():
        to_home(0).start()

    @pl.when(home == b)
    def _():
        c_r[b, spot] = c_s[q]

    own_gate.wait()
    own_part.wait()
    own_weights.wait()
    for k in range(1, bins):
        frm = (b + k) % bins
        remote(g_v.at[:, cols(frm)], g_t.at[frm], gs.at[frm], gr.at[frm], (frm, c)).wait_recv()
        remote(w_v.at[:, cols(frm)], w_t.at[frm], ws.at[frm], wr.at[frm], (frm, c)).wait_recv()
        remote(p_v.at[pl.ds(0, hg)], p_t.at[frm], ps.at[frm], pr.at[frm], (frm, c)).wait_recv()
        remote(bs_own, bs_t.at[frm], bss.at[frm], bsr.at[frm], (frm, c)).wait_recv()
    for bb in range(bins):
        for r in range(parts):
            same = (bb == b) & (b * parts + r == q)

            @pl.when(jnp.logical_not(same))
            def _():
                remote(
                    c_s.at[0], c_r.at[bb, pl.ds(r * own, own)], l3s.at[0], l3r.at[bb, r], (b, c)
                ).wait_recv()

    def to_next(j):
        return remote(v_s.at[j], v_n.at[j], vs.at[j], vr.at[j], (b, nxt))

    def full_step(j, carry):
        def one(bb, inner):
            ct[...] = c_r[bb, j].astype(F32)
            acc = [jnp.zeros((SUB, 128), F32) for _ in range(tokens // SUB)]
            for m in range(modes):
                d = gtab[j, m] * jnp.broadcast_to(ct[pl.ds(m, 1), :], (SUB, 128))
                a = wide(ta8, j, m)
                for t in range(tokens // SUB):
                    acc[t] = acc[t] + d
                    if t + 1 < tokens // SUB:
                        d = d * a
            conv = jnp.concatenate(acc, axis=0)
            gate = g_t[bb, :, lanes(j)].astype(F32)
            v_s[j, bb] = (w_t[bb, :, lanes(j)].astype(F32) + gate * conv).astype(BF16)
            return inner

        lax.fori_loop(0, bins, one, 0)
        to_next(j).start()
        return carry

    lax.fori_loop(0, hg, full_step, 0)

    def piece(j, to):
        return remote(
            o_s.at[j, to],
            out_h.at[0, :, lanes(b * hg + j)],
            os_.at[j, to],
            or_.at[j, b],
            (to, c),
        )

    def mix_step(j, carry):
        to_next(j).wait_recv()
        for bb in range(bins):
            w = p_t[bb, j]
            o = jnp.dot(w * low[...], v_s[j, bb], preferred_element_type=F32)
            o = o + jnp.dot(w * upp[...], v_n[j, bb], preferred_element_type=F32)
            o_f[2 * bb] = o[:half]
            o_f[2 * bb + 1] = o[half:]

        def deal(n, inner):
            to = (b + 1 + n) % bins
            for s in range(2):
                pick = jnp.broadcast_to(bs_t[to, pl.ds(s, 1), :], (half, 128))
                got = o_f[0]
                for src in range(1, 2 * bins):
                    got = jnp.where(pick == src, o_f[src], got)
                o_s[j, to, pl.ds(s * half, half), :] = got.astype(BF16)

            @pl.when(to != b)
            def _():
                piece(j, to).start()

            return inner

        lax.fori_loop(0, bins, deal, 0)
        pltpu.make_async_copy(o_s.at[j, b], out_h.at[0, :, lanes(b * hg + j)], oloc.at[3 + j]).start()
        return carry

    lax.fori_loop(0, hg, mix_step, 0)

    for k in range(1, near):
        to_near((q + k) % near).wait_send()
        to_home(k).wait_send()

    @pl.when(home != b)
    def _():
        to_home(0).wait_send()

    for k in range(1, groups):

        @pl.when(grp + k < groups)
        def _():
            to_later(k).wait_send()

    key_send.wait_send()
    id_send.wait_send()
    for k in range(1, bins):
        to = (b + k) % bins
        remote(g_v.at[:, cols(to)], g_t.at[b], gs.at[to], gr.at[b], (to, c)).wait_send()
        remote(w_v.at[:, cols(to)], w_t.at[b], ws.at[to], wr.at[b], (to, c)).wait_send()
        remote(p_v.at[pl.ds(to * hg, hg)], p_t.at[b], ps.at[to], pr.at[b], (to, c)).wait_send()
        remote(bs_own, bs_t.at[b], bss.at[to], bsr.at[b], (to, c)).wait_send()
    for j in range(hg):
        to_next(j).wait_send()
        pltpu.make_async_copy(o_s.at[j, b], out_h.at[0, :, lanes(b * hg + j)], oloc.at[3 + j]).wait()
        for k in range(1, bins):
            other = (b + k) % bins
            piece(j, other).wait_send()
            remote(
                o_s.at[j, other],
                out_h.at[0, :, lanes(other * hg + j)],
                os_.at[j, other],
                or_.at[j, other],
                (other, c),
            ).wait_recv()


def per_device(mesh_shape, x, gate, residues, rates, skip, queries, keys, ids, source):
    bins, ctx, near, groups, far_z, far_x = plan(mesh_shape)
    tokens, channels = x.shape[1:]
    modes = residues.shape[0]
    lg = channels // 128
    own = lg // near
    hg = lg // bins
    dims = (bins, ctx, near, groups, far_z, far_x, tokens, channels, modes)
    any_spec = pl.BlockSpec(memory_space=pl.ANY)
    vmem = pltpu.VMEM
    dma = pltpu.SemaphoreType.DMA
    scratch = [
        vmem((tokens, channels), BF16),
        vmem((tokens, channels), BF16),
        vmem((modes, channels), F32),
        vmem((modes, channels), F32),
        vmem((1, channels), F32),
        vmem((tokens, channels), BF16),
        vmem((tokens, channels), BF16),
        vmem((1, tokens), jnp.int32),
        vmem((tokens, 128), F32),
        vmem((lg, tokens // SUB, SUB, 128), F32),
        vmem((lg, modes, SUB, 128), F32),
        vmem((lg, modes, 128), F32),
        vmem((lg, modes, 128), F32),
        vmem((lg, modes, 128), F32),
        vmem((lg, modes, 128), F32),
        vmem((modes, 128), F32),
        vmem((lg, modes, 128), STATE),
        vmem((near, own, modes, 128), STATE),
        vmem((near, own, modes, 128), F32),
        vmem((own, modes, 128), STATE),
        vmem((groups, own, modes, 128), STATE),
        vmem((near, own, modes, 128), STATE),
        vmem((bins, hg, modes, 128), STATE),
        vmem((tokens, channels), BF16),
        vmem((lg, tokens, tokens), BF16),
        vmem((bins, tokens, hg * 128), BF16),
        vmem((bins, tokens, hg * 128), BF16),
        vmem((bins, hg, tokens, tokens), BF16),
        vmem((tokens, channels), BF16),
        vmem((SUB, 128), jnp.int32),
        vmem((SUB, 128), jnp.int32),
        vmem((SUB, 128), jnp.int32),
        vmem((bins, SUB, 128), jnp.int32),
        vmem((tokens, tokens), F32),
        vmem((tokens, tokens), BF16),
        vmem((tokens, tokens), BF16),
        vmem((hg, modes, SUB, 128), F32),
        vmem((hg, modes, 128), F32),
        vmem((modes, 128), F32),
        vmem((hg, bins, tokens, 128), BF16),
        vmem((hg, bins, tokens, 128), BF16),
        vmem((2 * bins, tokens // 2, 128), F32),
        vmem((hg, bins, tokens, 128), BF16),
        dma((8,)),
        dma((near,)), dma((near,)),
        dma((groups,)), dma((groups,)),
        dma((near,)), dma((bins, hg // own)),
        dma((bins,)), dma((bins,)),
        dma((bins,)), dma((bins,)),
        dma((bins,)), dma((bins,)),
        dma((bins,)), dma((bins,)),
        dma, dma,
        dma, dma,
        dma((hg,)), dma((hg,)),
        dma((hg, bins)), dma((hg, bins)),
        dma((3 + hg,)),
        pltpu.SemaphoreType.REGULAR,
        pltpu.SemaphoreType.REGULAR,
    ]
    return pl.pallas_call(
        functools.partial(kernel, dims),
        out_shape=jax.ShapeDtypeStruct((1, tokens, channels), BF16),
        in_specs=[any_spec] * 8 + [pl.BlockSpec(memory_space=pltpu.SMEM)],
        out_specs=any_spec,
        scratch_shapes=scratch,
        compiler_params=pltpu.CompilerParams(
            collective_id=0, has_side_effects=True, vmem_limit_bytes=40 * 1024 * 1024
        ),
        name="hybrid_pair",
    )(x, gate, residues, rates, skip.reshape(1, -1), queries, keys, ids, source)


def solution(mesh):
    rows = P("bins", "ctx", None)
    pairs = P("bins", "ctx")
    return jax.shard_map(
        functools.partial(per_device, dict(mesh.shape)),
        mesh=mesh,
        in_specs=(rows, rows, P(), P(), P(), rows, rows, pairs, pairs),
        out_specs=rows,
        check_vma=False,
    )
```

```python
import functools

import jax
import jax.numpy as jnp
from jax import lax
from jax.experimental import pallas as pl
from jax.experimental.pallas import tpu as pltpu
from jax.sharding import PartitionSpec as P

MESH = pl.DeviceIdType.MESH
HEAD_DIM = 128
SUB = 8
F32 = jnp.float32
BF16 = jnp.bfloat16
STATE = BF16


def plan(mesh_shape):
    bins, ctx = mesh_shape["bins"], mesh_shape["ctx"]
    near = 8 if ctx >= 64 else 2
    groups = ctx // near
    far_z = 4 if groups >= 16 else 2
    return bins, ctx, near, groups, far_z, groups // far_z


def kernel(
    dims,
    x_h, g_h, res_h, lam_h, skip_h, q_h, k_h, ids_h, bs_s,
    out_h,
    x_v, g_v, res_v, lam_v, skip_v, q_v, k_v, ids_v,
    xf, xs, pm, ta, ta16, ta32, ta64, et, e_s, e_r, pre, t_s, t_r, c_s, c_r,
    w_v, p_v, w_t, g_t, p_t, k_n, id_s, id_n, bs_own, bs_t, bias, low, upp,
    gtab, ta8, ct, v_s, v_n, o_f, o_s,
    loc, l1s, l1r, l2s, l2r, l3s, l3r, gs, gr, ws, wr, ps, pr, bss, bsr,
    ks, kr, ids_, idr, vs, vr, os_, or_, oloc, xl, home_sem, second_sem, third_sem,
):
    bins, ctx, near, groups, far_z, far_x, tokens, channels, modes = dims
    lane_groups = channels // 128
    own = lane_groups // near
    hg = lane_groups // bins
    width = hg * 128
    parts = hg // own
    chunk = tokens // SUB
    half = tokens // 2

    b = lax.axis_index("bins")
    c = lax.axis_index("ctx")
    grp = c // near
    q = c % near
    gx, gz = grp // far_z, grp % far_z
    home = (q * own) // hg
    nxt = (c + 1) % ctx

    def remote(src, dst, ss, rs, dev):
        return pltpu.make_async_remote_copy(
            src_ref=src, dst_ref=dst, send_sem=ss, recv_sem=rs, device_id=dev, device_id_type=MESH
        )

    def lanes(index):
        return pl.ds(pl.multiple_of(index * 128, 128), 128)

    def cols(index):
        return pl.ds(pl.multiple_of(index * width, 128), width)

    def partner(k):
        flip = near - 1 - k
        peer, bit = 0, 1
        while bit < near:
            mine, other = (q // bit) % 2, (flip // bit) % 2
            peer = peer + bit * (mine + other - 2 * mine * other)
            bit *= 2
        return peer

    def x_load(pair):
        some = pl.ds(pl.multiple_of(pair * own * 256, 128), own * 256)
        return pltpu.make_async_copy(x_h.at[0, :, some], x_v.at[:, some], xl.at[pair])

    loads = [
        pltpu.make_async_copy(s, d, loc.at[n])
        for n, (s, d) in enumerate(
            [(lam_h, lam_v), (g_h.at[0], g_v), (k_h.at[0], k_v), (res_h, res_v), (skip_h, skip_v),
             (q_h.at[0], q_v), (ids_h, ids_v)]
        )
    ]
    loads[0].start()
    for k in range(near // 2):
        x_load(partner(2 * k) // 2).start()
    loads[1].start()
    loads[2].start()

    bar = pltpu.get_barrier_semaphore()

    def greet(dev):
        pl.semaphore_signal(bar, inc=1, device_id=dev, device_id_type=MESH)

    def at(x, z):
        return (b, (x * far_z + z) * near + q)

    home_targets = [(home, grp * near + n) for n in range(near)]
    scanners = [[(bb, grp * near + b * parts + r) for r in range(parts)] for bb in range(bins)]
    count = (near - 1) + (bins - 1) + (far_x - 1)
    for k in range(1, near):
        greet((b, grp * near + (q + k) % near))
    for k in range(1, bins):
        greet(((b + k) % bins, c))

    @pl.when(c > 0)
    def _():
        greet((b, c - 1))

    count = count + jnp.where(c + 1 < ctx, 1, 0)
    row_devs = [at((gx + k) % far_x, gz) for k in range(1, far_x)]
    col_devs = [at(gx, (gz + k) % far_z) for k in (1, far_z - 1)]
    for dev in row_devs + col_devs:
        greet(dev)
    count = count + len(col_devs)

    with jax.named_scope("rates_load"):
        loads[0].wait()
    row = lax.broadcasted_iota(jnp.int32, (SUB, 128), 0)
    m1 = (row >= 1).astype(F32)
    m2 = (row >= 2).astype(F32)
    m4 = (row >= 4).astype(F32)

    def wide(ref, g, m):
        return jnp.broadcast_to(ref[g, pl.ds(m, 1), :], (SUB, 128))

    def states(g):
        rate = lam_v[:, lanes(g)]
        ta[g] = jnp.exp(-rate)
        ta16[g] = jnp.exp(rate * (-1.0 * chunk))
        ta32[g] = jnp.exp(rate * (-2.0 * chunk))
        ta64[g] = jnp.exp(rate * (-4.0 * chunk))
        xf[...] = x_v[:, lanes(g)].astype(F32)
        xt = [xf[pl.ds(t, SUB, stride=chunk), :] for t in range(chunk)]
        for t in range(chunk):
            xs[g, t] = xt[t]
        for m in range(modes):
            a = wide(ta, g, m)
            e = xt[0]
            for t in range(1, chunk):
                e = e * a + xt[t]
            e = e + (wide(ta16, g, m) * m1) * pltpu.roll(e, 1, 0)
            e = e + (wide(ta32, g, m) * m2) * pltpu.roll(e, 2, 0)
            e = e + (wide(ta64, g, m) * m4) * pltpu.roll(e, 4, 0)
            pm[g, m] = pltpu.roll(e, 1, 0) * m1
            et[pl.ds(m, 1), :] = e[SUB - 1 :, :]
        e_s[g] = et[...].astype(STATE)

    def to_near(peer):
        return remote(
            e_s.at[pl.ds(peer * own, own)], e_r.at[q], l1s.at[peer], l1r.at[q], (b, grp * near + peer)
        )

    def state_step(k, carry):
        peer = partner(k)

        @pl.when(k % 2 == 0)
        def _():
            x_load(peer // 2).wait()

        for j in range(own):
            states(peer * own + j)
        return carry

    def state_send_step(k, carry):
        carry = state_step(k, carry)
        peer = partner(k)

        @pl.when(peer != q)
        def _():
            to_near(peer).start()

        return carry

    lead = near - near // 4 if near > 4 else near // 2
    with jax.named_scope("first_states"):
        lax.fori_loop(0, lead, state_step, 0)
    def tell(sem, dev):
        pl.semaphore_signal(sem, inc=1, device_id=dev, device_id_type=MESH)

    with jax.named_scope("barrier"):
        pl.semaphore_wait(bar, count)
    for dev in row_devs + col_devs:
        tell(second_sem, dev)
    for k in range(lead):
        to_near(partner(k)).start()
    loads[2].wait()
    key_send = remote(k_v, k_n, ks, kr, (b, nxt))

    @pl.when(c + 1 < ctx)
    def _():
        key_send.start()

    loads[1].wait()
    for k in range(1, bins):
        to = (b + k) % bins
        remote(g_v.at[:, cols(to)], g_t.at[b], gs.at[to], gr.at[b], (to, c)).start()
    for load in loads[3:]:
        load.start()
    with jax.named_scope("last_states"):
        lax.fori_loop(lead, near, state_send_step, 0)

    e_r[q] = e_s[pl.ds(q * own, own)]

    for load in loads[3:]:
        load.wait()
    id_s[...] = jnp.broadcast_to(ids_v[...], (SUB, 128))
    id_send = remote(id_s, id_n, ids_, idr, (b, nxt))

    @pl.when(c + 1 < ctx)
    def _():
        id_send.start()

    block_row = jnp.where(row == 0, bs_s[0, 0], bs_s[0, 1])
    bs_own[...] = block_row
    bs_t[b] = block_row
    for k in range(1, bins):
        to = (b + k) % bins
        remote(bs_own, bs_t.at[b], bss.at[to], bsr.at[b], (to, c)).start()
    own_gate = pltpu.make_async_copy(g_v.at[:, cols(b)], g_t.at[b], oloc.at[0])
    own_gate.start()

    def values_here(g):
        xt = [xs[g, t] for t in range(chunk)]
        cur = res_v[:, lanes(g)]
        rate = ta[g]
        taps = []
        for t in range(chunk):
            taps.append(jnp.broadcast_to(jnp.sum(cur, axis=0, keepdims=True), (SUB, 128)))
            cur = cur * rate
            if t == 0:
                et[...] = cur
        skip = jnp.broadcast_to(skip_v[:, lanes(g)], (SUB, 128))
        y = []
        for t in range(chunk):
            acc = (skip + taps[0]) * xt[t]
            for k in range(1, t + 1):
                acc = acc + taps[k] * xt[t - k]
            y.append(acc)
        for m in range(modes):
            a = wide(ta, g, m)
            d = jnp.broadcast_to(et[pl.ds(m, 1), :], (SUB, 128)) * pm[g, m]
            for t in range(chunk):
                y[t] = y[t] + d
                if t + 1 < chunk:
                    d = d * a
        for t in range(chunk):
            xf[pl.ds(t, SUB, stride=chunk), :] = y[t]
        w_v[:, lanes(g)] = (g_v[:, lanes(g)].astype(F32) * xf[...]).astype(BF16)

    def values_step(n, carry):
        to = (b + 1 + n) % bins

        def one(j, inner):
            values_here(to * hg + j)
            return inner

        lax.fori_loop(0, hg, one, 0)

        @pl.when(to != b)
        def _():
            remote(w_v.at[:, cols(to)], w_t.at[b], ws.at[to], wr.at[b], (to, c)).start()

        return carry

    with jax.named_scope("values"):
        lax.fori_loop(0, bins // 2, values_step, 0)
    with jax.named_scope("second"):
        pl.semaphore_wait(second_sem, len(row_devs) + len(col_devs))
    for dev in col_devs:
        tell(third_sem, dev)
    with jax.named_scope("values"):
        lax.fori_loop(bins // 2, bins, values_step, 0)
    own_part = pltpu.make_async_copy(w_v.at[:, cols(b)], w_t.at[b], oloc.at[1])
    own_part.start()

    with jax.named_scope("near_states"):
        for k in range(1, near):
            peer = (q + k) % near
            remote(e_s.at[pl.ds(0, own)], e_r.at[peer], l1s.at[peer], l1r.at[peer], (b, c)).wait_recv()
    step, leap = [], []
    for j in range(own):
        rate = lam_v[:, lanes(q * own + j)]
        step.append(jnp.exp(rate * (-1.0 * tokens)))
        leap.append(jnp.exp(rate * (-1.0 * tokens * near)))
        acc = jnp.zeros((modes, 128), F32)
        for n in range(near):
            pre[n, j] = acc
            acc = step[j] * acc + e_r[n, j].astype(F32)
        t_s[j] = acc.astype(STATE)

    def to_group(x, z):
        other = x * far_z + z
        return remote(t_s, t_r.at[grp], l2s.at[other], l2r.at[grp], at(x, z))

    def send_totals(ready):
        for z in range(far_z):
            opposite = (z - gz + far_z) % far_z == 2
            for x in range(far_x):
                last = opposite & (x != gx)

                @pl.when((x * far_z + z > grp) & (last != ready))
                def _():
                    to_group(x, z).start()

    send_totals(True)
    with jax.named_scope("third"):
        pl.semaphore_wait(third_sem, len(col_devs))
    send_totals(False)

    @pl.when(c > 0)
    def _():
        with jax.named_scope("keys"):
            key_send.wait_recv()
            id_send.wait_recv()

    @pl.when(c == 0)
    def _():
        k_n[...] = jnp.zeros_like(k_n)
        id_n[...] = jnp.zeros_like(id_n)

    t_idx = lax.broadcasted_iota(jnp.int32, (tokens, tokens), 0)
    u_idx = lax.broadcasted_iota(jnp.int32, (tokens, tokens), 1)
    lower = u_idx <= t_idx
    low[...] = lower.astype(F32).astype(BF16)
    upp[...] = (u_idx > t_idx).astype(F32).astype(BF16)
    id_row = jnp.broadcast_to(id_s[0:1, :].astype(F32), (tokens, tokens))
    id_col = id_row.T
    shut = jnp.where(c == 0, 65536.0, 0.0)
    id_before = jnp.broadcast_to(id_n[0:1, :].astype(F32), (tokens, tokens)) + shut
    id_key = jnp.where(lower, id_row, id_before)
    bias[...] = jnp.where(id_key == id_col, 0.0, -1e30)

    def weights_step(n, carry):
        to = (b + 1 + n) % bins
        for j in range(hg):
            h = to * hg + j
            query = q_v[:, lanes(h)]
            dn = (((1,), (1,)), ((), ()))
            s_own = lax.dot_general(query, k_v[:, lanes(h)], dn, preferred_element_type=F32)
            s_prev = lax.dot_general(query, k_n[:, lanes(h)], dn, preferred_element_type=F32)
            u_i = lax.broadcasted_iota(jnp.int32, (tokens, tokens), 1)
            t_i = lax.broadcasted_iota(jnp.int32, (tokens, tokens), 0)
            s = jnp.where(u_i <= t_i, s_own, s_prev) * HEAD_DIM ** (-0.5) + bias[...]
            e = jnp.exp(s - jnp.max(s, axis=1, keepdims=True))
            p_v[h] = (e * (1.0 / jnp.sum(e, axis=1, keepdims=True))).astype(BF16)

        @pl.when(to != b)
        def _():
            remote(p_v.at[pl.ds(to * hg, hg)], p_t.at[b], ps.at[to], pr.at[b], (to, c)).start()

        return carry

    with jax.named_scope("weights"):
        lax.fori_loop(0, bins, weights_step, 0)
    own_weights = pltpu.make_async_copy(p_v.at[pl.ds(b * hg, hg)], p_t.at[b], oloc.at[2])
    own_weights.start()

    def gate_from(frm):
        return remote(g_v.at[:, cols(frm)], g_t.at[frm], gs.at[frm], gr.at[frm], (frm, c))

    def part_from(frm):
        return remote(w_v.at[:, cols(frm)], w_t.at[frm], ws.at[frm], wr.at[frm], (frm, c))

    own_gate.wait()
    for k in range(1, bins):
        with jax.named_scope("gates"):
            gate_from((b + k) % bins).wait_recv()

    for bb in range(bins):
        for r in range(parts):

            @pl.when(jnp.logical_not((bb == b) & (b * parts + r == q)))
            def _():
                tell(home_sem, scanners[bb][r])

    ramp = (row + 1).astype(F32)

    def table_step(j, carry):
        g = b * hg + j
        ta8[j] = jnp.exp(lam_v[:, lanes(g)] * (-1.0 * SUB))
        for m in range(modes):
            rate = jnp.broadcast_to(lam_v[pl.ds(m, 1), lanes(g)], (SUB, 128))
            weight = jnp.broadcast_to(res_v[pl.ds(m, 1), lanes(g)], (SUB, 128))
            gtab[j, m] = weight * jnp.exp(-rate * ramp)
        return carry

    lax.fori_loop(0, hg, table_step, 0)

    def earlier(n, carry):
        remote(t_s, t_r.at[n], l2s.at[0], l2r.at[n], (b, c)).wait_recv()
        return tuple(leap[j] * carry[j] + t_r[n, j].astype(F32) for j in range(own))

    with jax.named_scope("totals"):
        start = lax.fori_loop(
            0, grp, earlier, tuple(jnp.zeros((modes, 128), F32) for _ in range(own))
        )
    for j in range(own):
        power = start[j]
        for n in range(near):
            c_s[n, j] = (pre[n, j] + power).astype(STATE)
            power = power * step[j]
    spot = pl.ds((q % parts) * own, own)

    def to_home(n):
        return remote(c_s.at[n], c_r.at[b, spot], l3s.at[n], l3r.at[b, q % parts], home_targets[n])

    with jax.named_scope("homes"):
        pl.semaphore_wait(home_sem, near - jnp.where(home == b, 1, 0))
    for n in range(near):
        to_self = (home == b) & (q == n)

        @pl.when(jnp.logical_not(to_self))
        def _():
            to_home(n).start()

        @pl.when(to_self)
        def _():
            c_r[b, spot] = c_s[n]

    own_part.wait()
    for k in range(1, bins):
        with jax.named_scope("parts"):
            part_from((b + k) % bins).wait_recv()
    for bb in range(bins):
        for r in range(parts):

            @pl.when(jnp.logical_not((bb == b) & (b * parts + r == q)))
            def _():
                with jax.named_scope("states_in"):
                    remote(
                        c_s.at[0], c_r.at[bb, pl.ds(r * own, own)], l3s.at[0], l3r.at[bb, r], (b, c)
                    ).wait_recv()

    def to_next(j):
        return remote(v_s.at[j], v_n.at[j], vs.at[j], vr.at[j], (b, nxt))

    def full_step(j, carry):
        def one(bb, inner):
            ct[...] = c_r[bb, j].astype(F32)
            acc = [jnp.zeros((SUB, 128), F32) for _ in range(tokens // SUB)]
            for m in range(modes):
                d = gtab[j, m] * jnp.broadcast_to(ct[pl.ds(m, 1), :], (SUB, 128))
                a = wide(ta8, j, m)
                for t in range(tokens // SUB):
                    acc[t] = acc[t] + d
                    if t + 1 < tokens // SUB:
                        d = d * a
            conv = jnp.concatenate(acc, axis=0)
            gate = g_t[bb, :, lanes(j)].astype(F32)
            v_s[j, bb] = (w_t[bb, :, lanes(j)].astype(F32) + gate * conv).astype(BF16)
            return inner

        lax.fori_loop(0, bins, one, 0)

        @pl.when(c + 1 < ctx)
        def _():
            to_next(j).start()

        return carry

    with jax.named_scope("full"):
        lax.fori_loop(0, hg, full_step, 0)

    own_weights.wait()
    for k in range(1, bins):
        frm = (b + k) % bins
        with jax.named_scope("weights_in"):
            remote(p_v.at[pl.ds(0, hg)], p_t.at[frm], ps.at[frm], pr.at[frm], (frm, c)).wait_recv()
            remote(bs_own, bs_t.at[frm], bss.at[frm], bsr.at[frm], (frm, c)).wait_recv()

    @pl.when(c == 0)
    def _():
        v_n[...] = jnp.zeros_like(v_n)

    def piece(j, to):
        return remote(
            o_s.at[j, to],
            out_h.at[0, :, lanes(b * hg + j)],
            os_.at[j, to],
            or_.at[j, b],
            (to, c),
        )

    def mix_step(j, carry):
        @pl.when(c > 0)
        def _():
            with jax.named_scope("values_in"):
                to_next(j).wait_recv()

        for bb in range(bins):
            w = p_t[bb, j]
            o = jnp.dot(w * low[...], v_s[j, bb], preferred_element_type=F32)
            o = o + jnp.dot(w * upp[...], v_n[j, bb], preferred_element_type=F32)
            o_f[2 * bb] = o[:half]
            o_f[2 * bb + 1] = o[half:]

        def deal(n, inner):
            to = (b + 1 + n) % bins
            for s in range(2):
                pick = jnp.broadcast_to(bs_t[to, pl.ds(s, 1), :], (half, 128))
                got = o_f[0]
                for src in range(1, 2 * bins):
                    got = jnp.where(pick == src, o_f[src], got)
                o_s[j, to, pl.ds(s * half, half), :] = got.astype(BF16)

            @pl.when(to != b)
            def _():
                piece(j, to).start()

            return inner

        lax.fori_loop(0, bins, deal, 0)
        pltpu.make_async_copy(o_s.at[j, b], out_h.at[0, :, lanes(b * hg + j)], oloc.at[3 + j]).start()
        return carry

    with jax.named_scope("attention"):
        lax.fori_loop(0, hg, mix_step, 0)

    for k in range(near):
        if k + 1 < near:
            to_near(partner(k)).wait_send()

        @pl.when(jnp.logical_not((home == b) & (q == k)))
        def _():
            to_home(k).wait_send()

    for z in range(far_z):
        for x in range(far_x):

            @pl.when(x * far_z + z > grp)
            def _():
                to_group(x, z).wait_send()

    @pl.when(c + 1 < ctx)
    def _():
        key_send.wait_send()
        id_send.wait_send()
        for j in range(hg):
            to_next(j).wait_send()

    for k in range(1, bins):
        to = (b + k) % bins
        remote(g_v.at[:, cols(to)], g_t.at[b], gs.at[to], gr.at[b], (to, c)).wait_send()
        remote(w_v.at[:, cols(to)], w_t.at[b], ws.at[to], wr.at[b], (to, c)).wait_send()
        remote(p_v.at[pl.ds(to * hg, hg)], p_t.at[b], ps.at[to], pr.at[b], (to, c)).wait_send()
        remote(bs_own, bs_t.at[b], bss.at[to], bsr.at[b], (to, c)).wait_send()
    for j in range(hg):
        pltpu.make_async_copy(o_s.at[j, b], out_h.at[0, :, lanes(b * hg + j)], oloc.at[3 + j]).wait()
        for k in range(1, bins):
            other = (b + k) % bins
            piece(j, other).wait_send()
            remote(
                o_s.at[j, other],
                out_h.at[0, :, lanes(other * hg + j)],
                os_.at[j, other],
                or_.at[j, other],
                (other, c),
            ).wait_recv()


def per_device(mesh_shape, x, gate, residues, rates, skip, queries, keys, ids, source):
    bins, ctx, near, groups, far_z, far_x = plan(mesh_shape)
    tokens, channels = x.shape[1:]
    modes = residues.shape[0]
    lg = channels // 128
    own = lg // near
    hg = lg // bins
    dims = (bins, ctx, near, groups, far_z, far_x, tokens, channels, modes)
    hbm = pl.BlockSpec(memory_space=pl.ANY)
    vmem = pltpu.VMEM
    dma = pltpu.SemaphoreType.DMA
    scratch = [
        vmem((tokens, channels), BF16),
        vmem((tokens, channels), BF16),
        vmem((modes, channels), F32),
        vmem((modes, channels), F32),
        vmem((1, channels), F32),
        vmem((tokens, channels), BF16),
        vmem((tokens, channels), BF16),
        vmem((1, tokens), jnp.int32),
        vmem((tokens, 128), F32),
        vmem((lg, tokens // SUB, SUB, 128), F32),
        vmem((lg, modes, SUB, 128), F32),
        vmem((lg, modes, 128), F32),
        vmem((lg, modes, 128), F32),
        vmem((lg, modes, 128), F32),
        vmem((lg, modes, 128), F32),
        vmem((modes, 128), F32),
        vmem((lg, modes, 128), STATE),
        vmem((near, own, modes, 128), STATE),
        vmem((near, own, modes, 128), F32),
        vmem((own, modes, 128), STATE),
        vmem((groups, own, modes, 128), STATE),
        vmem((near, own, modes, 128), STATE),
        vmem((bins, hg, modes, 128), STATE),
        vmem((tokens, channels), BF16),
        vmem((lg, tokens, tokens), BF16),
        vmem((bins, tokens, hg * 128), BF16),
        vmem((bins, tokens, hg * 128), BF16),
        vmem((bins, hg, tokens, tokens), BF16),
        vmem((tokens, channels), BF16),
        vmem((SUB, 128), jnp.int32),
        vmem((SUB, 128), jnp.int32),
        vmem((SUB, 128), jnp.int32),
        vmem((bins, SUB, 128), jnp.int32),
        vmem((tokens, tokens), F32),
        vmem((tokens, tokens), BF16),
        vmem((tokens, tokens), BF16),
        vmem((hg, modes, SUB, 128), F32),
        vmem((hg, modes, 128), F32),
        vmem((modes, 128), F32),
        vmem((hg, bins, tokens, 128), BF16),
        vmem((hg, bins, tokens, 128), BF16),
        vmem((2 * bins, tokens // 2, 128), F32),
        vmem((hg, bins, tokens, 128), BF16),
        dma((8,)),
        dma((near,)), dma((near,)),
        dma((groups,)), dma((groups,)),
        dma((near,)), dma((bins, hg // own)),
        dma((bins,)), dma((bins,)),
        dma((bins,)), dma((bins,)),
        dma((bins,)), dma((bins,)),
        dma((bins,)), dma((bins,)),
        dma, dma,
        dma, dma,
        dma((hg,)), dma((hg,)),
        dma((hg, bins)), dma((hg, bins)),
        dma((3 + hg,)),
        dma((near // 2,)),
    ] + [pltpu.SemaphoreType.REGULAR] * 3
    return pl.pallas_call(
        functools.partial(kernel, dims),
        out_shape=jax.ShapeDtypeStruct((1, tokens, channels), BF16),
        in_specs=[hbm] * 8 + [pl.BlockSpec(memory_space=pltpu.SMEM)],
        out_specs=hbm,
        scratch_shapes=scratch,
        compiler_params=pltpu.CompilerParams(
            collective_id=0, has_side_effects=True, vmem_limit_bytes=56 * 1024 * 1024
        ),
        name="hybrid_pair",
    )(x, gate, residues, rates, skip.reshape(1, -1), queries, keys, ids, source)


def solution(mesh):
    rows = P("bins", "ctx", None)
    pairs = P("bins", "ctx")
    return jax.shard_map(
        functools.partial(per_device, dict(mesh.shape)),
        mesh=mesh,
        in_specs=(rows, rows, P(), P(), P(), rows, rows, pairs, pairs),
        out_specs=rows,
        check_vma=False,
    )
```

```python
import functools

import jax
import jax.numpy as jnp
from jax import lax
from jax.experimental import pallas as pl
from jax.experimental.pallas import tpu as pltpu
from jax.sharding import PartitionSpec as P

MESH = pl.DeviceIdType.MESH
HEAD_DIM = 128
SUB = 8
F32 = jnp.float32
BF16 = jnp.bfloat16
STATE = BF16
LOCAL = 2


def plan(mesh_shape):
    bins, ctx = mesh_shape["bins"], mesh_shape["ctx"]
    near = 8 if ctx >= 64 else 2
    groups = ctx // near
    far_z = 4 if groups >= 16 else 2
    return bins, ctx, near, groups, far_z, groups // far_z


def kernel(
    dims,
    x_h, g_h, res_h, lam_h, skip_h, q_h, k_h, ids_h, bs_s,
    out_h,
    x_v, g_v, res_v, lam_v, skip_v, q_v, k_v, ids_v,
    xf, xs, pm, ta, ta16, ta32, ta64, et, e_s, e_r, pre, t_s, t_r, u_s, u_r, c_s, c_r,
    w_v, p_v, w_t, g_t, p_t, k_n, id_s, id_n, bs_own, bs_t, bias, low, upp,
    gtab, ta8, ct, v_s, v_n, o_f, o_s, g_n, w_n, c_p,
    loc, l1s, l1r, l2s, l2r, l4s, l4r, l3s, l3r, l3e, l3p, gs, gr, ws, wr, ps, pr, bss, bsr,
    ks, kr, ids_, idr, vs, vr, gns, gnr, wns, wnr, os_, or_, oloc, xl, home_sem, second_sem,
):
    bins, ctx, near, groups, far_z, far_x, tokens, channels, modes = dims
    lane_groups = channels // 128
    own = lane_groups // near
    hg = lane_groups // bins
    width = hg * 128
    parts = hg // own
    chunk = tokens // SUB
    half = tokens // 2

    b = lax.axis_index("bins")
    c = lax.axis_index("ctx")
    grp = c // near
    q = c % near
    gx, gz = grp // far_z, grp % far_z
    home, lot = q // parts, q % parts
    nxt = (c + 1) % ctx

    def remote(src, dst, ss, rs, dev):
        return pltpu.make_async_remote_copy(
            src_ref=src, dst_ref=dst, send_sem=ss, recv_sem=rs, device_id=dev, device_id_type=MESH
        )

    def lanes(index):
        return pl.ds(pl.multiple_of(index * 128, 128), 128)

    def cols(index):
        return pl.ds(pl.multiple_of(index * width, 128), width)

    def part_at(k):
        flip = near - 1 - k
        part, bit = 0, 1
        while bit < near:
            mine, other = (q // bit) % 2, (flip // bit) % 2
            part = part + bit * (mine + other - 2 * mine * other)
            bit *= 2
        return part

    def x_load(bin_):
        return pltpu.make_async_copy(x_h.at[0, :, cols(bin_)], x_v.at[:, cols(bin_)], xl.at[bin_])

    loads = [
        pltpu.make_async_copy(s, d, loc.at[n])
        for n, (s, d) in enumerate(
            [(lam_h, lam_v), (g_h.at[0], g_v), (k_h.at[0], k_v), (res_h, res_v), (skip_h, skip_v),
             (q_h.at[0], q_v), (ids_h, ids_v)]
        )
    ]
    loads[0].start()
    for k in range(0, near, parts):
        x_load(part_at(k) // parts).start()

    bar = pltpu.get_barrier_semaphore()

    def greet(dev):
        pl.semaphore_signal(bar, inc=1, device_id=dev, device_id_type=MESH)

    def at(x, z):
        return (b, (x * far_z + z) * near + q)

    def near_dev(n, bin_=b):
        return (bin_, grp * near + n)

    row_devs = [at((gx + k) % far_x, gz) for k in range(1, far_x)]
    col_devs = [at(gx, (gz + k) % far_z) for k in (1, far_z - 1)]
    for dev in col_devs + row_devs:
        greet(dev)
    for k in range(1, near):
        greet(near_dev((q + k) % near))
    count = (near - 1) + (bins - 1) + (far_x - 1)
    count = count + len(col_devs)
    for k in range(1, bins):
        greet(((b + k) % bins, c))

    @pl.when(c > 0)
    def _():
        greet((b, c - 1))

    count = count + jnp.where(c + 1 < ctx, 1, 0)
    to_next_group = (lot == parts - 1) & (grp + 1 < groups)
    count = count + jnp.where(to_next_group, 1, 0)

    @pl.when((q == 0) & (grp > 0))
    def _():
        for i in range(bins):
            greet((i, (grp - 1) * near + b * parts + parts - 1))

    with jax.named_scope("rates_load"):
        loads[0].wait()
    loads[1].start()
    loads[2].start()
    row = lax.broadcasted_iota(jnp.int32, (SUB, 128), 0)
    m1 = (row >= 1).astype(F32)
    m2 = (row >= 2).astype(F32)
    m4 = (row >= 4).astype(F32)

    def wide(ref, g, m):
        return jnp.broadcast_to(ref[g, pl.ds(m, 1), :], (SUB, 128))

    def states(g):
        rate = lam_v[:, lanes(g)]
        ta[g] = jnp.exp(-rate)
        ta16[g] = jnp.exp(rate * (-1.0 * chunk))
        ta32[g] = jnp.exp(rate * (-2.0 * chunk))
        ta64[g] = jnp.exp(rate * (-4.0 * chunk))
        xf[...] = x_v[:, lanes(g)].astype(F32)
        xt = [xf[pl.ds(t, SUB, stride=chunk), :] for t in range(chunk)]
        for t in range(chunk):
            xs[g, t] = xt[t]
        for m in range(modes):
            a = wide(ta, g, m)
            e = xt[0]
            for t in range(1, chunk):
                e = e * a + xt[t]
            e = e + (wide(ta16, g, m) * m1) * pltpu.roll(e, 1, 0)
            e = e + (wide(ta32, g, m) * m2) * pltpu.roll(e, 2, 0)
            e = e + (wide(ta64, g, m) * m4) * pltpu.roll(e, 4, 0)
            pm[g, m] = pltpu.roll(e, 1, 0) * m1
            et[pl.ds(m, 1), :] = e[SUB - 1 :, :]
        e_s[g] = et[...].astype(STATE)

    def to_scan(part):
        return remote(
            e_s.at[pl.ds(part * own, own)], e_r.at[q], l1s.at[part], l1r.at[q], near_dev(part)
        )

    def send_states(k):
        @pl.when(part_at(k) != q)
        def _():
            to_scan(part_at(k)).start()

    def state_step(k, carry):
        @pl.when(k % parts == 0)
        def _():
            x_load(part_at(k) // parts).wait()

        for j in range(own):
            states(part_at(k) * own + j)
        return carry

    def state_send_step(k, carry):
        carry = state_step(k, carry)
        send_states(k)
        return carry

    lead = near - near // 4 if near > 4 else near // 2
    with jax.named_scope("first_states"):
        lax.fori_loop(0, lead, state_step, 0)
    def tell(sem, dev):
        pl.semaphore_signal(sem, inc=1, device_id=dev, device_id_type=MESH)

    with jax.named_scope("barrier"):
        pl.semaphore_wait(bar, count)
    for dev in col_devs:
        tell(second_sem, dev)

    for k in range(lead):
        send_states(k)
    loads[2].wait()
    key_send = remote(k_v, k_n, ks, kr, (b, nxt))

    @pl.when(c + 1 < ctx)
    def _():
        key_send.start()

    loads[1].wait()

    def send_gates():
        for k in range(1, bins):
            to = (b + k) % bins
            remote(g_v.at[:, cols(to)], g_t.at[b], gs.at[to], gr.at[b], (to, c)).start()

    def send_part(to):
        remote(w_v.at[:, cols(to)], w_t.at[b], ws.at[to], wr.at[b], (to, c)).start()

    send_gates()

    for load in loads[3:]:
        load.start()
    with jax.named_scope("last_states"):
        lax.fori_loop(lead, near, state_send_step, 0)

    e_r[q] = e_s[pl.ds(q * own, own)]

    for load in loads[3:]:
        load.wait()
    id_s[...] = jnp.broadcast_to(ids_v[...], (SUB, 128))
    id_send = remote(id_s, id_n, ids_, idr, (b, nxt))

    @pl.when(c + 1 < ctx)
    def _():
        id_send.start()

    block_row = jnp.where(row == 0, bs_s[0, 0], bs_s[0, 1])
    bs_own[...] = block_row
    bs_t[b] = block_row
    for k in range(1, bins):
        to = (b + k) % bins
        remote(bs_own, bs_t.at[b], bss.at[to], bsr.at[b], (to, c)).start()
    def last_heads(bin_):
        return pl.ds(pl.multiple_of((bin_ * hg + hg - LOCAL) * 128, 128), LOCAL * 128)

    def pass_gate(n):
        src = g_v.at[:, last_heads(b)] if n is None else g_t.at[n, :, last_heads(0)]
        n = b if n is None else n
        return remote(src, g_n.at[n], gns.at[n], gnr.at[n], (b, nxt))

    def pass_part(n):
        src = w_v.at[:, last_heads(b)] if n is None else w_t.at[n, :, last_heads(0)]
        n = b if n is None else n
        return remote(src, w_n.at[n], wns.at[n], wnr.at[n], (b, nxt))

    own_gate = pltpu.make_async_copy(g_v.at[:, cols(b)], g_t.at[b], oloc.at[0])
    own_gate.start()

    def values_here(g):
        xt = [xs[g, t] for t in range(chunk)]
        cur = res_v[:, lanes(g)]
        rate = ta[g]
        taps = []
        for t in range(chunk):
            taps.append(jnp.broadcast_to(jnp.sum(cur, axis=0, keepdims=True), (SUB, 128)))
            cur = cur * rate
            if t == 0:
                et[...] = cur
        skip = jnp.broadcast_to(skip_v[:, lanes(g)], (SUB, 128))
        y = []
        for t in range(chunk):
            acc = (skip + taps[0]) * xt[t]
            for k in range(1, t + 1):
                acc = acc + taps[k] * xt[t - k]
            y.append(acc)
        for m in range(modes):
            a = wide(ta, g, m)
            d = jnp.broadcast_to(et[pl.ds(m, 1), :], (SUB, 128)) * pm[g, m]
            for t in range(chunk):
                y[t] = y[t] + d
                if t + 1 < chunk:
                    d = d * a
        for t in range(chunk):
            xf[pl.ds(t, SUB, stride=chunk), :] = y[t]
        w_v[:, lanes(g)] = (g_v[:, lanes(g)].astype(F32) * xf[...]).astype(BF16)

    def values_step(n, carry):
        to = (b + 1 + n) % bins

        def one(j, inner):
            values_here(to * hg + j)
            return inner

        lax.fori_loop(0, hg, one, 0)

        @pl.when(to != b)
        def _():
            send_part(to)

        return carry

    with jax.named_scope("values"):
        lax.fori_loop(0, bins, values_step, 0)
    own_part = pltpu.make_async_copy(w_v.at[:, cols(b)], w_t.at[b], oloc.at[1])
    own_part.start()

    with jax.named_scope("near_states"):
        for n in range(near):

            @pl.when(q != n)
            def _():
                remote(
                    e_s.at[pl.ds(0, own)], e_r.at[n], l1s.at[0], l1r.at[n], (b, c)
                ).wait_recv()

    step, leap = [], []
    for j in range(own):
        rate = lam_v[:, lanes(q * own + j)]
        step.append(jnp.exp(rate * (-1.0 * tokens)))
        leap.append(jnp.exp(rate * (-1.0 * tokens * near)))
        acc = jnp.zeros((modes, 128), F32)
        for n in range(near):
            pre[n, j] = acc
            acc = step[j] * acc + e_r[n, j].astype(F32)
        t_s[j] = acc.astype(STATE)

    def to_column(k):
        z = (gz + k) % far_z
        return remote(t_s, t_r.at[gz], l2s.at[z], l2r.at[gz], at(gx, z))

    t_r[gz] = t_s[...]
    with jax.named_scope("second"):
        pl.semaphore_wait(second_sem, len(col_devs))
    column_steps = [2, 1, 3] if far_z == 4 else list(range(1, far_z))
    for k in column_steps:
        to_column(k).start()

    def gate_from(frm):
        return remote(g_v.at[:, cols(frm)], g_t.at[frm], gs.at[frm], gr.at[frm], (frm, c))

    def part_from(frm):
        return remote(w_v.at[:, cols(frm)], w_t.at[frm], ws.at[frm], wr.at[frm], (frm, c))

    def take_gates():
        own_gate.wait()
        for k in range(1, bins):
            frm = (b + k) % bins
            with jax.named_scope("gates"):
                gate_from(frm).wait_recv()

        for i in range(bins):
            for r in range(parts):

                @pl.when(jnp.logical_not((i == b) & (b * parts + r == q)))
                def _():
                    tell(home_sem, near_dev(b * parts + r, i))

    def take_parts():
        @pl.when(c + 1 < ctx)
        def _():
            pass_gate(None).start()
            for k in range(1, bins):
                pass_gate((b + k) % bins).start()
            pass_part(None).start()

        own_part.wait()
        for k in range(1, bins):
            frm = (b + k) % bins
            with jax.named_scope("parts"):
                part_from(frm).wait_recv()

            @pl.when(c + 1 < ctx)
            def _():
                pass_part(frm).start()

    def take_weights():
        @pl.when(c > 0)
        def _():
            with jax.named_scope("keys"):
                key_send.wait_recv()
                id_send.wait_recv()

        @pl.when(c == 0)
        def _():
            k_n[...] = jnp.zeros_like(k_n)
            id_n[...] = jnp.zeros_like(id_n)

        t_idx = lax.broadcasted_iota(jnp.int32, (tokens, tokens), 0)
        u_idx = lax.broadcasted_iota(jnp.int32, (tokens, tokens), 1)
        lower = u_idx <= t_idx
        low[...] = lower.astype(F32).astype(BF16)
        upp[...] = (u_idx > t_idx).astype(F32).astype(BF16)
        id_row = jnp.broadcast_to(id_s[0:1, :].astype(F32), (tokens, tokens))
        id_col = id_row.T
        shut = jnp.where(c == 0, 65536.0, 0.0)
        id_before = jnp.broadcast_to(id_n[0:1, :].astype(F32), (tokens, tokens)) + shut
        id_key = jnp.where(lower, id_row, id_before)
        bias[...] = jnp.where(id_key == id_col, 0.0, -1e30)

        def weights_step(n, carry):
            to = (b + 1 + n) % bins
            for j in range(hg):
                h = to * hg + j
                query = q_v[:, lanes(h)]
                dn = (((1,), (1,)), ((), ()))
                s_own = lax.dot_general(query, k_v[:, lanes(h)], dn, preferred_element_type=F32)
                s_prev = lax.dot_general(query, k_n[:, lanes(h)], dn, preferred_element_type=F32)
                u_i = lax.broadcasted_iota(jnp.int32, (tokens, tokens), 1)
                t_i = lax.broadcasted_iota(jnp.int32, (tokens, tokens), 0)
                s = jnp.where(u_i <= t_i, s_own, s_prev) * HEAD_DIM ** (-0.5) + bias[...]
                e = jnp.exp(s - jnp.max(s, axis=1, keepdims=True))
                p_v[h] = (e * (1.0 / jnp.sum(e, axis=1, keepdims=True))).astype(BF16)

            @pl.when(to != b)
            def _():
                remote(p_v.at[pl.ds(to * hg, hg)], p_t.at[b], ps.at[to], pr.at[b], (to, c)).start()

            return carry

        with jax.named_scope("weights"):
            lax.fori_loop(0, bins, weights_step, 0)
        own_weights = pltpu.make_async_copy(p_v.at[pl.ds(b * hg, hg)], p_t.at[b], oloc.at[2])
        own_weights.start()

    waits_long = (gz == 0) & (q == 0) & (c > 0)

    @pl.when(jnp.logical_not(waits_long))
    def _():
        take_weights()

    take_gates()

    ramp = (row + 1).astype(F32)

    def table_step(j, carry):
        g = b * hg + j
        ta8[j] = jnp.exp(lam_v[:, lanes(g)] * (-1.0 * SUB))
        for m in range(modes):
            rate = jnp.broadcast_to(lam_v[pl.ds(m, 1), lanes(g)], (SUB, 128))
            weight = jnp.broadcast_to(res_v[pl.ds(m, 1), lanes(g)], (SUB, 128))
            gtab[j, m] = weight * jnp.exp(-rate * ramp)
        return carry

    lax.fori_loop(0, hg, table_step, 0)

    with jax.named_scope("totals"):
        for k in column_steps:
            z = (gz + k) % far_z
            remote(t_s, t_r.at[z], l2s.at[0], l2r.at[z], (b, c)).wait_recv()
    inside = []
    for j in range(own):
        whole_row, part_row = jnp.zeros((modes, 128), F32), jnp.zeros((modes, 128), F32)
        for z in range(far_z):
            total = t_r[z, j].astype(F32)
            whole_row = leap[j] * whole_row + total
            part_row = jnp.where(z < gz, leap[j] * part_row + total, part_row)
        inside.append(part_row)
        u_s[j] = whole_row.astype(STATE)

    def to_row(x):
        return remote(u_s, u_r.at[gx], l4s.at[x], l4r.at[gx], at(x, gz))

    for x in reversed(range(far_x)):

        @pl.when(x > gx)
        def _():
            to_row(x).start()

    def earlier(n, carry):
        remote(u_s, u_r.at[n], l4s.at[0], l4r.at[n], (b, c)).wait_recv()
        return tuple(
            row_leap[j] * carry[j] + u_r[n, j].astype(F32) for j in range(own)
        )

    row_leap = [jnp.exp(lam_v[:, lanes(q * own + j)] * (-1.0 * tokens * near * far_z)) for j in range(own)]
    with jax.named_scope("rows"):
        outside = lax.fori_loop(
            0, gx, earlier, tuple(jnp.zeros((modes, 128), F32) for _ in range(own))
        )
    reach = gz.astype(F32) * (-1.0 * tokens * near)
    start = [
        inside[j] + jnp.exp(lam_v[:, lanes(q * own + j)] * reach) * outside[j] for j in range(own)
    ]
    for j in range(own):
        power = start[j]
        for n in range(near):
            c_s[n, j] = (pre[n, j] + power).astype(STATE)
            power = power * step[j]
    spot = pl.ds(lot * own, own)

    def to_home(n):
        return remote(c_s.at[n], c_r.at[b, spot], l3s.at[n], l3r.at[b, lot], near_dev(n, home))

    def to_follower(n):
        return remote(c_s.at[n], c_p.at[b], l3e.at[n], l3p.at[b], near_dev(n + 1, home))

    def at_home(n):
        return (home == b) & (q == n)

    def has_follower(n):
        return to_next_group if n == near - 1 else (lot == parts - 1) & jnp.logical_not(at_home(n + 1))

    with jax.named_scope("homes"):
        pl.semaphore_wait(home_sem, near - jnp.where(home == b, 1, 0))
    for n in range(near):

        @pl.when(jnp.logical_not(at_home(n)))
        def _():
            to_home(n).start()

        @pl.when(at_home(n))
        def _():
            c_r[b, spot] = c_s[n]

    for n in range(near):

        @pl.when(has_follower(n))
        def _():
            to_follower(n).start()

        if n + 1 < near:

            @pl.when((lot == parts - 1) & at_home(n + 1))
            def _():
                c_p[b] = c_s[n]

    @pl.when(waits_long)
    def _():
        take_weights()

    take_parts()

    for i in range(bins):
        for r in range(parts):

            @pl.when(jnp.logical_not((i == b) & (b * parts + r == q)))
            def _():
                with jax.named_scope("states_in"):
                    remote(
                        c_s.at[0], c_r.at[i, pl.ds(r * own, own)], l3s.at[0], l3r.at[i, r], (b, c)
                    ).wait_recv()

    def to_next(j):
        return remote(v_s.at[j], v_n.at[j], vs.at[j], vr.at[j], (b, nxt))

    def whole(j, bb, states_of, part, gate):
        ct[...] = states_of.astype(F32)
        acc = [jnp.zeros((SUB, 128), F32) for _ in range(tokens // SUB)]
        for m in range(modes):
            d = gtab[j, m] * jnp.broadcast_to(ct[pl.ds(m, 1), :], (SUB, 128))
            a = wide(ta8, j, m)
            for t in range(tokens // SUB):
                acc[t] = acc[t] + d
                if t + 1 < tokens // SUB:
                    d = d * a
        conv = jnp.concatenate(acc, axis=0)
        return (part.astype(F32) + gate.astype(F32) * conv).astype(BF16)

    def full(j):
        def one(bb, inner):
            v_s[j, bb] = whole(j, bb, c_r[bb, j], w_t[bb, :, lanes(j)], g_t[bb, :, lanes(j)])
            return inner

        lax.fori_loop(0, bins, one, 0)

    def full_step(j, carry):
        full(j)

        @pl.when(c + 1 < ctx)
        def _():
            to_next(j).start()

        return carry

    with jax.named_scope("full"):
        lax.fori_loop(0, hg - LOCAL, full_step, 0)

    pltpu.make_async_copy(p_v.at[pl.ds(b * hg, hg)], p_t.at[b], oloc.at[2]).wait()
    for k in range(1, bins):
        frm = (b + k) % bins
        with jax.named_scope("weights_in"):
            remote(p_v.at[pl.ds(0, hg)], p_t.at[frm], ps.at[frm], pr.at[frm], (frm, c)).wait_recv()
            remote(bs_own, bs_t.at[frm], bss.at[frm], bsr.at[frm], (frm, c)).wait_recv()

    @pl.when(c == 0)
    def _():
        v_n[...] = jnp.zeros_like(v_n)

    def piece(j, to):
        return remote(
            o_s.at[j, to],
            out_h.at[0, :, lanes(b * hg + j)],
            os_.at[j, to],
            or_.at[j, b],
            (to, c),
        )

    def mix(j):
        for bb in range(bins):
            w = p_t[bb, j]
            o = jnp.dot(w * low[...], v_s[j, bb], preferred_element_type=F32)
            o = o + jnp.dot(w * upp[...], v_n[j, bb], preferred_element_type=F32)
            o_f[2 * bb] = o[:half]
            o_f[2 * bb + 1] = o[half:]

        def deal(n, inner):
            to = (b + 1 + n) % bins
            for s in range(2):
                pick = jnp.broadcast_to(bs_t[to, pl.ds(s, 1), :], (half, 128))
                got = o_f[0]
                for src in range(1, 2 * bins):
                    got = jnp.where(pick == src, o_f[src], got)
                o_s[j, to, pl.ds(s * half, half), :] = got.astype(BF16)

            @pl.when(to != b)
            def _():
                piece(j, to).start()

            return inner

        lax.fori_loop(0, bins, deal, 0)
        pltpu.make_async_copy(o_s.at[j, b], out_h.at[0, :, lanes(b * hg + j)], oloc.at[3 + j]).start()

    @pl.when(c > 0)
    def _():
        with jax.named_scope("halo_in"):
            for i in range(bins):
                pass_gate(i).wait_recv()
                pass_part(i).wait_recv()

                @pl.when((i != b) | (q != b * parts + parts - 1) | (q == 0))
                def _():
                    remote(c_s.at[0], c_p.at[i], l3e.at[0], l3p.at[i], (b, c)).wait_recv()

    def local_step(j, carry):
        full(j)

        @pl.when(c > 0)
        def _():
            def one(bb, inner):
                at_j = lanes(j - (hg - LOCAL))
                v_n[j, bb] = whole(
                    j, bb, c_p[bb, j - (hg - own)], w_n[bb, :, at_j], g_n[bb, :, at_j]
                )
                return inner

            lax.fori_loop(0, bins, one, 0)

        mix(j)
        return carry

    def halo_step(j, carry):
        @pl.when(c > 0)
        def _():
            with jax.named_scope("values_in"):
                to_next(j).wait_recv()

        mix(j)
        return carry

    with jax.named_scope("attention_last"):
        lax.fori_loop(hg - LOCAL, hg, local_step, 0)
    with jax.named_scope("attention"):
        lax.fori_loop(0, hg - LOCAL, halo_step, 0)

    for n in range(near):

        @pl.when(q != n)
        def _():
            to_scan(n).wait_send()

        @pl.when(jnp.logical_not(at_home(n)))
        def _():
            to_home(n).wait_send()

        @pl.when(has_follower(n))
        def _():
            to_follower(n).wait_send()

    for k in column_steps:
        to_column(k).wait_send()
    for x in range(far_x):

        @pl.when(x > gx)
        def _():
            to_row(x).wait_send()

    @pl.when(c + 1 < ctx)
    def _():
        key_send.wait_send()
        id_send.wait_send()
        for j in range(hg - LOCAL):
            to_next(j).wait_send()
        for i in range(bins):
            pass_gate(i).wait_send()
            pass_part(i).wait_send()

    for k in range(1, bins):
        to = (b + k) % bins
        remote(g_v.at[:, cols(to)], g_t.at[b], gs.at[to], gr.at[b], (to, c)).wait_send()
        remote(w_v.at[:, cols(to)], w_t.at[b], ws.at[to], wr.at[b], (to, c)).wait_send()
        remote(p_v.at[pl.ds(to * hg, hg)], p_t.at[b], ps.at[to], pr.at[b], (to, c)).wait_send()
        remote(bs_own, bs_t.at[b], bss.at[to], bsr.at[b], (to, c)).wait_send()
    for j in range(hg):
        pltpu.make_async_copy(o_s.at[j, b], out_h.at[0, :, lanes(b * hg + j)], oloc.at[3 + j]).wait()
        for k in range(1, bins):
            other = (b + k) % bins
            piece(j, other).wait_send()
            remote(
                o_s.at[j, other],
                out_h.at[0, :, lanes(other * hg + j)],
                os_.at[j, other],
                or_.at[j, other],
                (other, c),
            ).wait_recv()


def per_device(mesh_shape, x, gate, residues, rates, skip, queries, keys, ids, source):
    bins, ctx, near, groups, far_z, far_x = plan(mesh_shape)
    tokens, channels = x.shape[1:]
    modes = residues.shape[0]
    lg = channels // 128
    own = lg // near
    hg = lg // bins
    dims = (bins, ctx, near, groups, far_z, far_x, tokens, channels, modes)
    hbm = pl.BlockSpec(memory_space=pl.ANY)
    vmem = pltpu.VMEM
    dma = pltpu.SemaphoreType.DMA
    scratch = [
        vmem((tokens, channels), BF16),
        vmem((tokens, channels), BF16),
        vmem((modes, channels), F32),
        vmem((modes, channels), F32),
        vmem((1, channels), F32),
        vmem((tokens, channels), BF16),
        vmem((tokens, channels), BF16),
        vmem((1, tokens), jnp.int32),
        vmem((tokens, 128), F32),
        vmem((lg, tokens // SUB, SUB, 128), F32),
        vmem((lg, modes, SUB, 128), F32),
        vmem((lg, modes, 128), F32),
        vmem((lg, modes, 128), F32),
        vmem((lg, modes, 128), F32),
        vmem((lg, modes, 128), F32),
        vmem((modes, 128), F32),
        vmem((lg, modes, 128), STATE),
        vmem((near, own, modes, 128), STATE),
        vmem((near, own, modes, 128), F32),
        vmem((own, modes, 128), STATE),
        vmem((far_z, own, modes, 128), STATE),
        vmem((own, modes, 128), STATE),
        vmem((far_x, own, modes, 128), STATE),
        vmem((near, own, modes, 128), STATE),
        vmem((bins, hg, modes, 128), STATE),
        vmem((tokens, channels), BF16),
        vmem((lg, tokens, tokens), BF16),
        vmem((bins, tokens, hg * 128), BF16),
        vmem((bins, tokens, hg * 128), BF16),
        vmem((bins, hg, tokens, tokens), BF16),
        vmem((tokens, channels), BF16),
        vmem((SUB, 128), jnp.int32),
        vmem((SUB, 128), jnp.int32),
        vmem((SUB, 128), jnp.int32),
        vmem((bins, SUB, 128), jnp.int32),
        vmem((tokens, tokens), F32),
        vmem((tokens, tokens), BF16),
        vmem((tokens, tokens), BF16),
        vmem((hg, modes, SUB, 128), F32),
        vmem((hg, modes, 128), F32),
        vmem((modes, 128), F32),
        vmem((hg, bins, tokens, 128), BF16),
        vmem((hg, bins, tokens, 128), BF16),
        vmem((2 * bins, tokens // 2, 128), F32),
        vmem((hg, bins, tokens, 128), BF16),
        vmem((bins, tokens, LOCAL * 128), BF16),
        vmem((bins, tokens, LOCAL * 128), BF16),
        vmem((bins, own, modes, 128), STATE),
        dma((8,)),
        dma((near,)), dma((near,)),
        dma((far_z,)), dma((far_z,)),
        dma((far_x,)), dma((far_x,)),
        dma((near,)), dma((bins, hg // own)),
        dma((near,)), dma((bins,)),
        dma((bins,)), dma((bins,)),
        dma((bins,)), dma((bins,)),
        dma((bins,)), dma((bins,)),
        dma((bins,)), dma((bins,)),
        dma, dma,
        dma, dma,
        dma((hg,)), dma((hg,)),
        dma((bins,)), dma((bins,)),
        dma((bins,)), dma((bins,)),
        dma((hg, bins)), dma((hg, bins)),
        dma((3 + hg,)),
        dma((bins,)),
    ] + [pltpu.SemaphoreType.REGULAR] * 2
    return pl.pallas_call(
        functools.partial(kernel, dims),
        out_shape=jax.ShapeDtypeStruct((1, tokens, channels), BF16),
        in_specs=[hbm] * 8 + [pl.BlockSpec(memory_space=pltpu.SMEM)],
        out_specs=hbm,
        scratch_shapes=scratch,
        compiler_params=pltpu.CompilerParams(
            collective_id=0, has_side_effects=True, vmem_limit_bytes=56 * 1024 * 1024
        ),
        name="hybrid_pair",
    )(x, gate, residues, rates, skip.reshape(1, -1), queries, keys, ids, source)


def solution(mesh):
    rows = P("bins", "ctx", None)
    pairs = P("bins", "ctx")
    return jax.shard_map(
        functools.partial(per_device, dict(mesh.shape)),
        mesh=mesh,
        in_specs=(rows, rows, P(), P(), P(), rows, rows, pairs, pairs),
        out_specs=rows,
        check_vma=False,
    )
```

```python
import functools

import jax
import jax.numpy as jnp
from jax import lax
from jax.experimental import pallas as pl
from jax.experimental.pallas import tpu as pltpu
from jax.sharding import PartitionSpec as P

MESH = pl.DeviceIdType.MESH
HEAD_DIM = 128
SUB = 8
F32 = jnp.float32
BF16 = jnp.bfloat16
STATE = BF16
LOCAL = 1


def plan(mesh_shape):
    bins, ctx = mesh_shape["bins"], mesh_shape["ctx"]
    near = 8 if ctx >= 64 else 2
    groups = ctx // near
    far_z = 4 if groups >= 16 else 2
    return bins, ctx, near, groups, far_z, groups // far_z


def kernel(
    dims,
    x_h, g_h, res_h, lam_h, skip_h, q_h, k_h, ids_h, bs_s,
    out_h,
    x_v, g_v, res_v, lam_v, skip_v, q_v, k_v, ids_v,
    xf, xs, pm, ta, ta16, ta32, ta64, et, e_s, e_r, pre, t_s, t_r, u_s, u_r, c_s, c_r,
    w_v, p_v, w_t, g_t, p_t, k_n, id_s, id_n, bs_own, bs_t, bias, low, upp,
    gtab, ta8, ct, v_s, v_n, o_f, o_s, g_n, w_n, c_p,
    loc, l1s, l1r, l2s, l2r, l4s, l4r, l3s, l3r, l3e, l3p, gs, gr, ws, wr, ps, pr, bss, bsr,
    ks, kr, ids_, idr, vs, vr, gns, gnr, wns, wnr, os_, or_, oloc, xl, home_sem, second_sem,
):
    bins, ctx, near, groups, far_z, far_x, tokens, channels, modes = dims
    lane_groups = channels // 128
    own = lane_groups // near
    hg = lane_groups // bins
    width = hg * 128
    parts = hg // own
    chunk = tokens // SUB
    half = tokens // 2

    b = lax.axis_index("bins")
    c = lax.axis_index("ctx")
    grp = c // near
    q = c % near
    gx, gz = grp // far_z, grp % far_z
    home, lot = q // parts, q % parts
    nxt = (c + 1) % ctx

    def remote(src, dst, ss, rs, dev):
        return pltpu.make_async_remote_copy(
            src_ref=src, dst_ref=dst, send_sem=ss, recv_sem=rs, device_id=dev, device_id_type=MESH
        )

    def whole_of(ref, ss, rs):
        return remote(ref, ref, ss.at[0], rs.at[0], (b, c))

    def lanes(index):
        return pl.ds(pl.multiple_of(index * 128, 128), 128)

    def cols(index):
        return pl.ds(pl.multiple_of(index * width, 128), width)

    def part_at(k):
        flip = near - 1 - k
        part, bit = 0, 1
        while bit < near:
            mine, other = (q // bit) % 2, (flip // bit) % 2
            part = part + bit * (mine + other - 2 * mine * other)
            bit *= 2
        return part

    def x_load(bin_):
        return pltpu.make_async_copy(x_h.at[0, :, cols(bin_)], x_v.at[:, cols(bin_)], xl.at[bin_])

    loads = [
        pltpu.make_async_copy(s, d, loc.at[n])
        for n, (s, d) in enumerate(
            [(lam_h, lam_v), (g_h.at[0], g_v), (k_h.at[0], k_v), (res_h, res_v), (skip_h, skip_v),
             (q_h.at[0], q_v), (ids_h, ids_v)]
        )
    ]
    loads[0].start()
    for k in range(0, near, parts):
        x_load(part_at(k) // parts).start()

    bar = pltpu.get_barrier_semaphore()

    def greet(dev):
        pl.semaphore_signal(bar, inc=1, device_id=dev, device_id_type=MESH)

    def at(x, z):
        return (b, (x * far_z + z) * near + q)

    def near_dev(n, bin_=b):
        return (bin_, grp * near + n)

    row_devs = [at((gx + k) % far_x, gz) for k in range(1, far_x)]
    col_devs = [at(gx, (gz + k) % far_z) for k in (1, far_z - 1)]
    for dev in col_devs + row_devs:
        greet(dev)
    for k in range(1, near):
        greet(near_dev((q + k) % near))
    count = (near - 1) + (bins - 1) + (far_x - 1)
    count = count + len(col_devs)
    for k in range(1, bins):
        greet(((b + k) % bins, c))

    @pl.when(c > 0)
    def _():
        greet((b, c - 1))

    count = count + jnp.where(c + 1 < ctx, 1, 0)
    to_next_group = (lot == parts - 1) & (grp + 1 < groups)
    count = count + jnp.where(to_next_group, 1, 0)

    @pl.when((q == 0) & (grp > 0))
    def _():
        for i in range(bins):
            greet((i, (grp - 1) * near + b * parts + parts - 1))

    with jax.named_scope("rates_load"):
        loads[0].wait()
    loads[1].start()
    loads[2].start()
    row = lax.broadcasted_iota(jnp.int32, (SUB, 128), 0)
    m1 = (row >= 1).astype(F32)
    m2 = (row >= 2).astype(F32)
    m4 = (row >= 4).astype(F32)

    def wide(ref, g, m):
        return jnp.broadcast_to(ref[g, pl.ds(m, 1), :], (SUB, 128))

    def states(g):
        rate = lam_v[:, lanes(g)]
        ta[g] = jnp.exp(-rate)
        ta16[g] = jnp.exp(rate * (-1.0 * chunk))
        ta32[g] = jnp.exp(rate * (-2.0 * chunk))
        ta64[g] = jnp.exp(rate * (-4.0 * chunk))
        xf[...] = x_v[:, lanes(g)].astype(F32)
        xt = [xf[pl.ds(t, SUB, stride=chunk), :] for t in range(chunk)]
        for t in range(chunk):
            xs[g, t] = xt[t]
        for m in range(modes):
            a = wide(ta, g, m)
            e = xt[0]
            for t in range(1, chunk):
                e = e * a + xt[t]
            e = e + (wide(ta16, g, m) * m1) * pltpu.roll(e, 1, 0)
            e = e + (wide(ta32, g, m) * m2) * pltpu.roll(e, 2, 0)
            e = e + (wide(ta64, g, m) * m4) * pltpu.roll(e, 4, 0)
            pm[g, m] = pltpu.roll(e, 1, 0) * m1
            et[pl.ds(m, 1), :] = e[SUB - 1 :, :]
        e_s[g] = et[...].astype(STATE)

    def to_scan(part):
        return remote(
            e_s.at[pl.ds(part * own, own)], e_r.at[q], l1s.at[0], l1r.at[0], near_dev(part)
        )

    def send_states(k):
        @pl.when(part_at(k) != q)
        def _():
            to_scan(part_at(k)).start()

    def state_step(k, carry):
        @pl.when(k % parts == 0)
        def _():
            x_load(part_at(k) // parts).wait()

        for j in range(own):
            states(part_at(k) * own + j)
        return carry

    def state_send_step(k, carry):
        carry = state_step(k, carry)
        send_states(k)
        return carry

    lead = near - near // 4 if near > 4 else near // 2
    with jax.named_scope("first_states"):
        lax.fori_loop(0, lead, state_step, 0)
    def tell(sem, dev):
        pl.semaphore_signal(sem, inc=1, device_id=dev, device_id_type=MESH)

    with jax.named_scope("barrier"):
        pl.semaphore_wait(bar, count)
    for dev in col_devs:
        tell(second_sem, dev)

    for k in range(lead):
        send_states(k)
    loads[2].wait()
    key_send = remote(k_v, k_n, ks, kr, (b, nxt))

    @pl.when(c + 1 < ctx)
    def _():
        key_send.start()

    loads[1].wait()

    def send_gates():
        for k in range(1, bins):
            to = (b + k) % bins
            remote(g_v.at[:, cols(to)], g_t.at[b], gs.at[0], gr.at[0], (to, c)).start()

    def send_part(to):
        remote(w_v.at[:, cols(to)], w_t.at[b], ws.at[0], wr.at[0], (to, c)).start()

    send_gates()

    for load in loads[3:]:
        load.start()
    with jax.named_scope("last_states"):
        lax.fori_loop(lead, near, state_send_step, 0)

    e_r[q] = e_s[pl.ds(q * own, own)]

    for load in loads[3:]:
        load.wait()
    id_s[...] = jnp.broadcast_to(ids_v[...], (SUB, 128))
    id_send = remote(id_s, id_n, ids_, idr, (b, nxt))

    @pl.when(c + 1 < ctx)
    def _():
        id_send.start()

    block_row = jnp.where(row == 0, bs_s[0, 0], bs_s[0, 1])
    bs_own[...] = block_row
    bs_t[b] = block_row
    for k in range(1, bins):
        to = (b + k) % bins
        remote(bs_own, bs_t.at[b], bss.at[0], bsr.at[0], (to, c)).start()
    def last_heads(bin_):
        return pl.ds(pl.multiple_of((bin_ * hg + hg - LOCAL) * 128, 128), LOCAL * 128)

    def pass_gate(n):
        src = g_v.at[:, last_heads(b)] if n is None else g_t.at[n, :, last_heads(0)]
        n = b if n is None else n
        return remote(src, g_n.at[n], gns.at[0], gnr.at[0], (b, nxt))

    def pass_part(n):
        src = w_v.at[:, last_heads(b)] if n is None else w_t.at[n, :, last_heads(0)]
        n = b if n is None else n
        return remote(src, w_n.at[n], wns.at[0], wnr.at[0], (b, nxt))

    own_gate = pltpu.make_async_copy(g_v.at[:, cols(b)], g_t.at[b], oloc.at[0])
    own_gate.start()

    def values_here(g):
        xt = [xs[g, t] for t in range(chunk)]
        cur = res_v[:, lanes(g)]
        rate = ta[g]
        taps = []
        for t in range(chunk):
            taps.append(jnp.broadcast_to(jnp.sum(cur, axis=0, keepdims=True), (SUB, 128)))
            cur = cur * rate
            if t == 0:
                et[...] = cur
        skip = jnp.broadcast_to(skip_v[:, lanes(g)], (SUB, 128))
        y = []
        for t in range(chunk):
            acc = (skip + taps[0]) * xt[t]
            for k in range(1, t + 1):
                acc = acc + taps[k] * xt[t - k]
            y.append(acc)
        for m in range(modes):
            a = wide(ta, g, m)
            d = jnp.broadcast_to(et[pl.ds(m, 1), :], (SUB, 128)) * pm[g, m]
            for t in range(chunk):
                y[t] = y[t] + d
                if t + 1 < chunk:
                    d = d * a
        for t in range(chunk):
            xf[pl.ds(t, SUB, stride=chunk), :] = y[t]
        w_v[:, lanes(g)] = (g_v[:, lanes(g)].astype(F32) * xf[...]).astype(BF16)

    def values_step(n, carry):
        to = (b + 1 + n) % bins

        def one(j, inner):
            values_here(to * hg + j)
            return inner

        lax.fori_loop(0, hg, one, 0)

        @pl.when(to != b)
        def _():
            send_part(to)

        return carry

    with jax.named_scope("values"):
        lax.fori_loop(0, bins, values_step, 0)
    own_part = pltpu.make_async_copy(w_v.at[:, cols(b)], w_t.at[b], oloc.at[1])
    own_part.start()

    with jax.named_scope("near_states"):
        whole_of(e_r.at[pl.ds(0, near - 1)], l1s, l1r).wait_recv()
    step, leap = [], []
    for j in range(own):
        rate = lam_v[:, lanes(q * own + j)]
        step.append(jnp.exp(rate * (-1.0 * tokens)))
        leap.append(jnp.exp(rate * (-1.0 * tokens * near)))
        acc = jnp.zeros((modes, 128), F32)
        for n in range(near):
            pre[n, j] = acc
            acc = step[j] * acc + e_r[n, j].astype(F32)
        t_s[j] = acc.astype(STATE)

    def to_column(k):
        z = (gz + k) % far_z
        return remote(t_s, t_r.at[gz], l2s.at[0], l2r.at[0], at(gx, z))

    t_r[gz] = t_s[...]
    with jax.named_scope("second"):
        pl.semaphore_wait(second_sem, len(col_devs))
    column_steps = [2, 1, 3] if far_z == 4 else list(range(1, far_z))
    for k in column_steps:
        to_column(k).start()

    def gate_from(frm):
        return remote(g_v.at[:, cols(frm)], g_t.at[frm], gs.at[0], gr.at[0], (frm, c))

    def part_from(frm):
        return remote(w_v.at[:, cols(frm)], w_t.at[frm], ws.at[0], wr.at[0], (frm, c))

    def take_gates():
        own_gate.wait()
        with jax.named_scope("gates"):
            whole_of(g_t.at[pl.ds(0, bins - 1)], gs, gr).wait_recv()

        for i in range(bins):
            for r in range(parts):

                @pl.when(jnp.logical_not((i == b) & (b * parts + r == q)))
                def _():
                    tell(home_sem, near_dev(b * parts + r, i))

    def take_parts():
        @pl.when(c + 1 < ctx)
        def _():
            pass_gate(None).start()
            for k in range(1, bins):
                pass_gate((b + k) % bins).start()
            pass_part(None).start()

        own_part.wait()
        with jax.named_scope("parts"):
            whole_of(w_t.at[pl.ds(0, bins - 1)], ws, wr).wait_recv()

        @pl.when(c + 1 < ctx)
        def _():
            for k in range(1, bins):
                pass_part((b + k) % bins).start()

    def take_weights():
        @pl.when(c > 0)
        def _():
            with jax.named_scope("keys"):
                key_send.wait_recv()
                id_send.wait_recv()

        @pl.when(c == 0)
        def _():
            k_n[...] = jnp.zeros_like(k_n)
            id_n[...] = jnp.zeros_like(id_n)

        t_idx = lax.broadcasted_iota(jnp.int32, (tokens, tokens), 0)
        u_idx = lax.broadcasted_iota(jnp.int32, (tokens, tokens), 1)
        lower = u_idx <= t_idx
        low[...] = lower.astype(F32).astype(BF16)
        upp[...] = (u_idx > t_idx).astype(F32).astype(BF16)
        id_row = jnp.broadcast_to(id_s[0:1, :].astype(F32), (tokens, tokens))
        id_col = id_row.T
        shut = jnp.where(c == 0, 65536.0, 0.0)
        id_before = jnp.broadcast_to(id_n[0:1, :].astype(F32), (tokens, tokens)) + shut
        id_key = jnp.where(lower, id_row, id_before)
        bias[...] = jnp.where(id_key == id_col, 0.0, -1e30)

        def weights_step(n, carry):
            to = (b + 1 + n) % bins
            for j in range(hg):
                h = to * hg + j
                query = q_v[:, lanes(h)]
                dn = (((1,), (1,)), ((), ()))
                s_own = lax.dot_general(query, k_v[:, lanes(h)], dn, preferred_element_type=F32)
                s_prev = lax.dot_general(query, k_n[:, lanes(h)], dn, preferred_element_type=F32)
                u_i = lax.broadcasted_iota(jnp.int32, (tokens, tokens), 1)
                t_i = lax.broadcasted_iota(jnp.int32, (tokens, tokens), 0)
                s = jnp.where(u_i <= t_i, s_own, s_prev) * HEAD_DIM ** (-0.5) + bias[...]
                e = jnp.exp(s - jnp.max(s, axis=1, keepdims=True))
                p_v[h] = (e * (1.0 / jnp.sum(e, axis=1, keepdims=True))).astype(BF16)

            @pl.when(to != b)
            def _():
                remote(p_v.at[pl.ds(to * hg, hg)], p_t.at[b], ps.at[0], pr.at[0], (to, c)).start()

            return carry

        with jax.named_scope("weights"):
            lax.fori_loop(0, bins, weights_step, 0)
        own_weights = pltpu.make_async_copy(p_v.at[pl.ds(b * hg, hg)], p_t.at[b], oloc.at[2])
        own_weights.start()

    waits_long = (gz == 0) & (q == 0) & (c > 0)

    @pl.when(jnp.logical_not(waits_long))
    def _():
        take_weights()

    take_gates()

    ramp = (row + 1).astype(F32)

    def table_step(j, carry):
        g = b * hg + j
        ta8[j] = jnp.exp(lam_v[:, lanes(g)] * (-1.0 * SUB))
        for m in range(modes):
            rate = jnp.broadcast_to(lam_v[pl.ds(m, 1), lanes(g)], (SUB, 128))
            weight = jnp.broadcast_to(res_v[pl.ds(m, 1), lanes(g)], (SUB, 128))
            gtab[j, m] = weight * jnp.exp(-rate * ramp)
        return carry

    lax.fori_loop(0, hg, table_step, 0)

    with jax.named_scope("totals"):
        whole_of(t_r.at[pl.ds(0, far_z - 1)], l2s, l2r).wait_recv()
    inside = []
    for j in range(own):
        whole_row, part_row = jnp.zeros((modes, 128), F32), jnp.zeros((modes, 128), F32)
        for z in range(far_z):
            total = t_r[z, j].astype(F32)
            whole_row = leap[j] * whole_row + total
            part_row = jnp.where(z < gz, leap[j] * part_row + total, part_row)
        inside.append(part_row)
        u_s[j] = whole_row.astype(STATE)

    def to_row(x):
        return remote(u_s, u_r.at[gx], l4s.at[x], l4r.at[gx], at(x, gz))

    for x in reversed(range(far_x)):

        @pl.when(x > gx)
        def _():
            to_row(x).start()

    def earlier(n, carry):
        remote(u_s, u_r.at[n], l4s.at[0], l4r.at[n], (b, c)).wait_recv()
        return tuple(
            row_leap[j] * carry[j] + u_r[n, j].astype(F32) for j in range(own)
        )

    row_leap = [jnp.exp(lam_v[:, lanes(q * own + j)] * (-1.0 * tokens * near * far_z)) for j in range(own)]
    with jax.named_scope("rows"):
        outside = lax.fori_loop(
            0, gx, earlier, tuple(jnp.zeros((modes, 128), F32) for _ in range(own))
        )
    reach = gz.astype(F32) * (-1.0 * tokens * near)
    start = [
        inside[j] + jnp.exp(lam_v[:, lanes(q * own + j)] * reach) * outside[j] for j in range(own)
    ]
    for j in range(own):
        power = start[j]
        for n in range(near):
            c_s[n, j] = (pre[n, j] + power).astype(STATE)
            power = power * step[j]
    spot = pl.ds(lot * own, own)

    def to_home(n):
        return remote(c_s.at[n], c_r.at[b, spot], l3s.at[0], l3r.at[0], near_dev(n, home))

    def to_follower(n):
        return remote(c_s.at[n], c_p.at[b], l3e.at[0], l3p.at[0], near_dev(n + 1, home))

    def at_home(n):
        return (home == b) & (q == n)

    def has_follower(n):
        return to_next_group if n == near - 1 else (lot == parts - 1) & jnp.logical_not(at_home(n + 1))

    with jax.named_scope("homes"):
        pl.semaphore_wait(home_sem, near - jnp.where(home == b, 1, 0))
    for n in range(near):

        @pl.when(jnp.logical_not(at_home(n)))
        def _():
            to_home(n).start()

        @pl.when(at_home(n))
        def _():
            c_r[b, spot] = c_s[n]

    for n in range(near):

        @pl.when(has_follower(n))
        def _():
            to_follower(n).start()

        if n + 1 < near:

            @pl.when((lot == parts - 1) & at_home(n + 1))
            def _():
                c_p[b] = c_s[n]

    whole_of(e_r.at[pl.ds(0, near - 1)], l1s, l1r).wait_send()
    whole_of(t_r.at[pl.ds(0, far_z - 1)], l2s, l2r).wait_send()

    @pl.when(c + 1 < ctx)
    def _():
        key_send.wait_send()
        id_send.wait_send()

    whole_of(g_t.at[pl.ds(0, bins - 1)], gs, gr).wait_send()
    whole_of(bs_t.at[pl.ds(0, bins - 1)], bss, bsr).wait_send()

    @pl.when(waits_long)
    def _():
        take_weights()

    take_parts()

    @pl.when(home == b)
    def _():
        with jax.named_scope("states_in"):
            whole_of(c_s.at[pl.ds(0, near - 1)], l3s, l3r).wait_recv()

    @pl.when(home != b)
    def _():
        with jax.named_scope("states_in"):
            whole_of(c_s, l3s, l3r).wait_recv()

    def to_next(j):
        return remote(v_s.at[j], v_n.at[j], vs.at[j], vr.at[j], (b, nxt))

    def whole(j, bb, states_of, part, gate):
        ct[...] = states_of.astype(F32)
        acc = [jnp.zeros((SUB, 128), F32) for _ in range(tokens // SUB)]
        for m in range(modes):
            d = gtab[j, m] * jnp.broadcast_to(ct[pl.ds(m, 1), :], (SUB, 128))
            a = wide(ta8, j, m)
            for t in range(tokens // SUB):
                acc[t] = acc[t] + d
                if t + 1 < tokens // SUB:
                    d = d * a
        conv = jnp.concatenate(acc, axis=0)
        return (part.astype(F32) + gate.astype(F32) * conv).astype(BF16)

    def full(j):
        def one(bb, inner):
            v_s[j, bb] = whole(j, bb, c_r[bb, j], w_t[bb, :, lanes(j)], g_t[bb, :, lanes(j)])
            return inner

        lax.fori_loop(0, bins, one, 0)

    def full_step(j, carry):
        full(j)

        @pl.when(c + 1 < ctx)
        def _():
            to_next(j).start()

        return carry

    with jax.named_scope("full"):
        lax.fori_loop(0, hg - LOCAL, full_step, 0)

        def own_step(j, carry):
            full(j)
            return carry

        lax.fori_loop(hg - LOCAL, hg, own_step, 0)

    pltpu.make_async_copy(p_v.at[pl.ds(b * hg, hg)], p_t.at[b], oloc.at[2]).wait()
    with jax.named_scope("weights_in"):
        whole_of(p_t.at[pl.ds(0, bins - 1)], ps, pr).wait_recv()
        whole_of(bs_t.at[pl.ds(0, bins - 1)], bss, bsr).wait_recv()

    @pl.when(c == 0)
    def _():
        v_n[...] = jnp.zeros_like(v_n)

    def piece(j, to):
        return remote(
            o_s.at[j, to],
            out_h.at[0, :, lanes(b * hg + j)],
            os_.at[0],
            or_.at[0],
            (to, c),
        )

    def own_piece(j):
        return pltpu.make_async_copy(o_s.at[j, b], out_h.at[0, :, lanes(b * hg + j)], oloc.at[3 + j])

    def mix(j):
        for bb in range(bins):
            w = p_t[bb, j]
            o = jnp.dot(w * low[...], v_s[j, bb], preferred_element_type=F32)
            o = o + jnp.dot(w * upp[...], v_n[j, bb], preferred_element_type=F32)
            o_f[2 * bb] = o[:half]
            o_f[2 * bb + 1] = o[half:]

        def deal(n, inner):
            to = (b + jnp.where(n == 0, bins // 2, jnp.where(n <= bins // 2 - 1, n, n + 1))) % bins
            for s in range(2):
                pick = jnp.broadcast_to(bs_t[to, pl.ds(s, 1), :], (half, 128))
                got = o_f[0]
                for src in range(1, 2 * bins):
                    got = jnp.where(pick == src, o_f[src], got)
                o_s[j, to, pl.ds(s * half, half), :] = got.astype(BF16)

            @pl.when(to != b)
            def _():
                piece(j, to).start()

            return inner

        lax.fori_loop(0, bins, deal, 0)
        own_piece(j).start()

    @pl.when(c > 0)
    def _():
        with jax.named_scope("gates_before"):
            whole_of(g_n, gns, gnr).wait_recv()
        with jax.named_scope("parts_before"):
            whole_of(w_n, wns, wnr).wait_recv()
        self_follows = (q == b * parts + parts - 1) & (q > 0)

        @pl.when(self_follows)
        def _():
            with jax.named_scope("states_before"):
                whole_of(c_p.at[pl.ds(0, bins - 1)], l3e, l3p).wait_recv()

        @pl.when(jnp.logical_not(self_follows))
        def _():
            with jax.named_scope("states_before"):
                whole_of(c_p, l3e, l3p).wait_recv()

    def local_step(j, carry):
        @pl.when(c > 0)
        def _():
            def one(bb, inner):
                at_j = lanes(j - (hg - LOCAL))
                v_n[j, bb] = whole(
                    j, bb, c_p[bb, j - (hg - own)], w_n[bb, :, at_j], g_n[bb, :, at_j]
                )
                return inner

            lax.fori_loop(0, bins, one, 0)

        mix(j)
        return carry

    def halo_step(j, carry):
        @pl.when(c > 0)
        def _():
            with jax.named_scope("values_in"):
                to_next(j).wait_recv()

        mix(j)
        return carry

    with jax.named_scope("attention_last"):
        lax.fori_loop(hg - LOCAL, hg, local_step, 0)
    @pl.when(home == b)
    def _():
        whole_of(c_s.at[pl.ds(0, near - 1)], l3s, l3r).wait_send()

    @pl.when(home != b)
    def _():
        whole_of(c_s, l3s, l3r).wait_send()

    followers = near - 1 - jnp.where((home == b) & (q > 0), 1, 0) + jnp.where(to_next_group, 1, 0)
    for n in range(max(near - 2, 1), near + 1):

        @pl.when((lot == parts - 1) & (followers == n))
        def _():
            whole_of(c_s.at[pl.ds(0, n)], l3e, l3p).wait_send()

    for x in range(far_x):

        @pl.when(x > gx)
        def _():
            to_row(x).wait_send()

    whole_of(w_t.at[pl.ds(0, bins - 1)], ws, wr).wait_send()
    whole_of(p_t.at[pl.ds(0, bins - 1)], ps, pr).wait_send()

    with jax.named_scope("attention"):
        lax.fori_loop(0, hg - LOCAL, halo_step, 0)

    with jax.named_scope("last_sends"):

        @pl.when(c + 1 < ctx)
        def _():
            for j in range(hg - LOCAL):
                to_next(j).wait_send()
            whole_of(g_n, gns, gnr).wait_send()
            whole_of(w_n, wns, wnr).wait_send()

    for j in list(range(hg - LOCAL, hg)) + list(range(hg - LOCAL)):
        with jax.named_scope("out_own"):
            own_piece(j).wait()
    with jax.named_scope("out_send"):
        whole_of(o_s.at[:, pl.ds(0, bins - 1)], os_, or_).wait_send()
    with jax.named_scope("out_in"):
        others = out_h.at[0, pl.ds(0, tokens * (bins - 1) // bins)]
        whole_of(others, os_, or_).wait_recv()


def per_device(mesh_shape, x, gate, residues, rates, skip, queries, keys, ids, source):
    bins, ctx, near, groups, far_z, far_x = plan(mesh_shape)
    tokens, channels = x.shape[1:]
    modes = residues.shape[0]
    lg = channels // 128
    own = lg // near
    hg = lg // bins
    dims = (bins, ctx, near, groups, far_z, far_x, tokens, channels, modes)
    hbm = pl.BlockSpec(memory_space=pl.ANY)
    vmem = pltpu.VMEM
    dma = pltpu.SemaphoreType.DMA
    scratch = [
        vmem((tokens, channels), BF16),
        vmem((tokens, channels), BF16),
        vmem((modes, channels), F32),
        vmem((modes, channels), F32),
        vmem((1, channels), F32),
        vmem((tokens, channels), BF16),
        vmem((tokens, channels), BF16),
        vmem((1, tokens), jnp.int32),
        vmem((tokens, 128), F32),
        vmem((lg, tokens // SUB, SUB, 128), F32),
        vmem((lg, modes, SUB, 128), F32),
        vmem((lg, modes, 128), F32),
        vmem((lg, modes, 128), F32),
        vmem((lg, modes, 128), F32),
        vmem((lg, modes, 128), F32),
        vmem((modes, 128), F32),
        vmem((lg, modes, 128), STATE),
        vmem((near, own, modes, 128), STATE),
        vmem((near, own, modes, 128), F32),
        vmem((own, modes, 128), STATE),
        vmem((far_z, own, modes, 128), STATE),
        vmem((own, modes, 128), STATE),
        vmem((far_x, own, modes, 128), STATE),
        vmem((near, own, modes, 128), STATE),
        vmem((bins, hg, modes, 128), STATE),
        vmem((tokens, channels), BF16),
        vmem((lg, tokens, tokens), BF16),
        vmem((bins, tokens, hg * 128), BF16),
        vmem((bins, tokens, hg * 128), BF16),
        vmem((bins, hg, tokens, tokens), BF16),
        vmem((tokens, channels), BF16),
        vmem((SUB, 128), jnp.int32),
        vmem((SUB, 128), jnp.int32),
        vmem((SUB, 128), jnp.int32),
        vmem((bins, SUB, 128), jnp.int32),
        vmem((tokens, tokens), F32),
        vmem((tokens, tokens), BF16),
        vmem((tokens, tokens), BF16),
        vmem((hg, modes, SUB, 128), F32),
        vmem((hg, modes, 128), F32),
        vmem((modes, 128), F32),
        vmem((hg, bins, tokens, 128), BF16),
        vmem((hg, bins, tokens, 128), BF16),
        vmem((2 * bins, tokens // 2, 128), F32),
        vmem((hg, bins, tokens, 128), BF16),
        vmem((bins, tokens, LOCAL * 128), BF16),
        vmem((bins, tokens, LOCAL * 128), BF16),
        vmem((bins, own, modes, 128), STATE),
        dma((8,)),
        dma((1,)), dma((1,)),
        dma((1,)), dma((1,)),
        dma((far_x,)), dma((far_x,)),
        dma((1,)), dma((1,)),
        dma((1,)), dma((1,)),
        dma((1,)), dma((1,)),
        dma((1,)), dma((1,)),
        dma((1,)), dma((1,)),
        dma((1,)), dma((1,)),
        dma, dma,
        dma, dma,
        dma((hg,)), dma((hg,)),
        dma((1,)), dma((1,)),
        dma((1,)), dma((1,)),
        dma((1,)), dma((1,)),
        dma((3 + hg,)),
        dma((bins,)),
    ] + [pltpu.SemaphoreType.REGULAR] * 2
    return pl.pallas_call(
        functools.partial(kernel, dims),
        out_shape=jax.ShapeDtypeStruct((1, tokens, channels), BF16),
        in_specs=[hbm] * 8 + [pl.BlockSpec(memory_space=pltpu.SMEM)],
        out_specs=hbm,
        scratch_shapes=scratch,
        compiler_params=pltpu.CompilerParams(
            collective_id=0, has_side_effects=True, vmem_limit_bytes=56 * 1024 * 1024
        ),
        name="hybrid_pair",
    )(x, gate, residues, rates, skip.reshape(1, -1), queries, keys, ids, source)


def solution(mesh):
    rows = P("bins", "ctx", None)
    pairs = P("bins", "ctx")
    return jax.shard_map(
        functools.partial(per_device, dict(mesh.shape)),
        mesh=mesh,
        in_specs=(rows, rows, P(), P(), P(), rows, rows, pairs, pairs),
        out_specs=rows,
        check_vma=False,
    )
```

```python
import functools

import jax
import jax.numpy as jnp
from jax import lax
from jax.experimental import pallas as pl
from jax.experimental.pallas import tpu as pltpu
from jax.sharding import PartitionSpec as P

MESH = pl.DeviceIdType.MESH
HEAD_DIM = 128
SUB = 8
F32 = jnp.float32
BF16 = jnp.bfloat16
STATE = BF16
LOCAL = 1


def plan(mesh_shape):
    bins, ctx = mesh_shape["bins"], mesh_shape["ctx"]
    near = 8 if ctx >= 64 else 2
    groups = ctx // near
    far_z = 4 if groups >= 16 else 2
    return bins, ctx, near, groups, far_z, groups // far_z


def kernel(
    dims,
    x_h, g_h, res_h, lam_h, skip_h, q_h, k_h, ids_h, bs_s,
    out_h,
    x_v, g_v, res_v, lam_v, skip_v, q_v, k_v, ids_v,
    xf, xs, pm, ta, ta16, ta32, ta64, et, e_s, e_r, pre, t_s, t_r, u_s, u_r, c_s, c_r,
    w_v, p_v, w_t, g_t, p_t, k_n, id_s, id_n, bs_own, bs_t, bias, low, upp,
    gtab, ta8, ct, v_s, v_n, o_f, o_s, g_n, w_n, c_p,
    loc, l1s, l1r, l2s, l2r, l4s, l4r, l3s, l3r, l3e, l3p, gs, gr, ws, wr, ps, pr, bss, bsr,
    ks, kr, ids_, idr, vs, vr, gns, gnr, wns, wnr, os_, or_, oloc, xl, home_sem, peer_sem, second_sem, nigh_sem, afar_sem,
):
    bins, ctx, near, groups, far_z, far_x, tokens, channels, modes = dims
    lane_groups = channels // 128
    own = lane_groups // near
    hg = lane_groups // bins
    width = hg * 128
    parts = hg // own
    chunk = tokens // SUB
    half = tokens // 2

    b = lax.axis_index("bins")
    c = lax.axis_index("ctx")
    grp = c // near
    q = c % near
    gx, gz = grp // far_z, grp % far_z
    home, lot = q // parts, q % parts
    nxt = (c + 1) % ctx

    def remote(src, dst, ss, rs, dev):
        return pltpu.make_async_remote_copy(
            src_ref=src, dst_ref=dst, send_sem=ss, recv_sem=rs, device_id=dev, device_id_type=MESH
        )

    def whole_of(ref, ss, rs):
        return remote(ref, ref, ss.at[0], rs.at[0], (b, c))

    def lanes(index):
        return pl.ds(pl.multiple_of(index * 128, 128), 128)

    def cols(index):
        return pl.ds(pl.multiple_of(index * width, 128), width)

    def part_at(k):
        flip = near - 1 - k
        part, bit = 0, 1
        while bit < near:
            mine, other = (q // bit) % 2, (flip // bit) % 2
            part = part + bit * (mine + other - 2 * mine * other)
            bit *= 2
        return part

    def x_load(bin_):
        return pltpu.make_async_copy(x_h.at[0, :, cols(bin_)], x_v.at[:, cols(bin_)], xl.at[bin_])

    loads = [
        pltpu.make_async_copy(s, d, loc.at[n])
        for n, (s, d) in enumerate(
            [(lam_h, lam_v), (g_h.at[0], g_v), (k_h.at[0], k_v), (res_h, res_v), (skip_h, skip_v),
             (q_h.at[0], q_v), (ids_h, ids_v)]
        )
    ]
    loads[0].start()
    for k in range(0, near, parts):
        x_load(part_at(k) // parts).start()

    bar = pltpu.get_barrier_semaphore()

    def greet(dev):
        pl.semaphore_signal(bar, inc=1, device_id=dev, device_id_type=MESH)

    def at(x, z):
        return (b, (x * far_z + z) * near + q)

    def near_dev(n, bin_=b):
        return (bin_, grp * near + n)

    heard = {0: (), 1: (0, 2), 2: (0, 1, 3), 3: (0, 2)}
    row_devs = [at((gx + k) % far_x, gz) for k in range(1, far_x)]
    for z in range(far_z):
        ears = [other for other in range(far_z) if z in heard[other]]

        @pl.when(gz == z)
        def _():
            for other in ears:
                greet(at(gx, other))

    for dev in row_devs:
        greet(dev)
    for k in range(1, near):
        greet(near_dev((q + k) % near))
    count = (near - 1) + (bins - 1) + (far_x - 1)
    count = count + sum(
        jnp.where(gz == z, len([other for other in heard[z] if other < far_z]), 0) for z in range(far_z)
    )
    for k in range(1, bins):
        greet(((b + k) % bins, c))

    @pl.when(c > 0)
    def _():
        greet((b, c - 1))

    count = count + jnp.where(c + 1 < ctx, 1, 0)
    to_next_group = (lot == parts - 1) & (grp + 1 < groups)
    count = count + jnp.where(to_next_group, 1, 0)

    @pl.when((q == 0) & (grp > 0))
    def _():
        for i in range(bins):
            greet((i, (grp - 1) * near + b * parts + parts - 1))

    with jax.named_scope("rates_load"):
        loads[0].wait()
    loads[1].start()
    loads[2].start()
    row = lax.broadcasted_iota(jnp.int32, (SUB, 128), 0)
    m1 = (row >= 1).astype(F32)
    m2 = (row >= 2).astype(F32)
    m4 = (row >= 4).astype(F32)

    def wide(ref, g, m):
        return jnp.broadcast_to(ref[g, pl.ds(m, 1), :], (SUB, 128))

    def states(g):
        rate = lam_v[:, lanes(g)]
        ta[g] = jnp.exp(-rate)
        ta16[g] = jnp.exp(rate * (-1.0 * chunk))
        ta32[g] = jnp.exp(rate * (-2.0 * chunk))
        ta64[g] = jnp.exp(rate * (-4.0 * chunk))
        xf[...] = x_v[:, lanes(g)].astype(F32)
        xt = [xf[pl.ds(t, SUB, stride=chunk), :] for t in range(chunk)]
        for t in range(chunk):
            xs[g, t] = xt[t]
        for m in range(modes):
            a = wide(ta, g, m)
            e = xt[0]
            for t in range(1, chunk):
                e = e * a + xt[t]
            e = e + (wide(ta16, g, m) * m1) * pltpu.roll(e, 1, 0)
            e = e + (wide(ta32, g, m) * m2) * pltpu.roll(e, 2, 0)
            e = e + (wide(ta64, g, m) * m4) * pltpu.roll(e, 4, 0)
            pm[g, m] = pltpu.roll(e, 1, 0) * m1
            et[pl.ds(m, 1), :] = e[SUB - 1 :, :]
        e_s[g] = et[...].astype(STATE)

    def to_scan(part):
        return remote(
            e_s.at[pl.ds(part * own, own)], e_r.at[q], l1s.at[0], l1r.at[0], near_dev(part)
        )

    def send_states(k):
        @pl.when(part_at(k) != q)
        def _():
            to_scan(part_at(k)).start()

    def state_step(k, carry):
        @pl.when(k % parts == 0)
        def _():
            x_load(part_at(k) // parts).wait()

        for j in range(own):
            states(part_at(k) * own + j)
        return carry

    def state_send_step(k, carry):
        carry = state_step(k, carry)
        send_states(k)
        return carry

    lead = near
    with jax.named_scope("first_states"):
        lax.fori_loop(0, lead, state_step, 0)
    def tell(sem, dev):
        pl.semaphore_signal(sem, inc=1, device_id=dev, device_id_type=MESH)

    with jax.named_scope("barrier"):
        pl.semaphore_wait(bar, count)
    for z in (1, 2, 3):
        if z < far_z:

            @pl.when(gz == z)
            def _():
                tell(afar_sem if z == 2 else nigh_sem, at(gx, 0))
                if z == 2 and far_z == 4:
                    tell(second_sem, at(gx, 1))
                    tell(second_sem, at(gx, 3))


    for k in range(lead):
        send_states(k)
    for k in range(1, bins):
        tell(peer_sem, ((b + k) % bins, c))
    loads[2].wait()
    key_send = remote(k_v, k_n, ks, kr, (b, nxt))

    @pl.when(c + 1 < ctx)
    def _():
        key_send.start()

    loads[1].wait()

    def send_gates():
        for k in range(1, bins):
            to = (b + k) % bins
            remote(g_v.at[:, cols(to)], g_t.at[b], gs.at[0], gr.at[0], (to, c)).start()

    def send_part(to):
        remote(w_v.at[:, cols(to)], w_t.at[b], ws.at[0], wr.at[0], (to, c)).start()

    send_gates()

    for load in loads[3:]:
        load.start()
    with jax.named_scope("last_states"):
        lax.fori_loop(lead, near, state_send_step, 0)

    e_r[q] = e_s[pl.ds(q * own, own)]

    for load in loads[3:]:
        load.wait()
    id_s[...] = jnp.broadcast_to(ids_v[...], (SUB, 128))
    id_send = remote(id_s, id_n, ids_, idr, (b, nxt))

    @pl.when(c + 1 < ctx)
    def _():
        id_send.start()

    block_row = jnp.where(row == 0, bs_s[0, 0], bs_s[0, 1])
    bs_own[...] = block_row
    bs_t[b] = block_row
    for k in range(1, bins):
        to = (b + k) % bins
        remote(bs_own, bs_t.at[b], bss.at[0], bsr.at[0], (to, c)).start()
    def last_heads(bin_):
        return pl.ds(pl.multiple_of((bin_ * hg + hg - LOCAL) * 128, 128), LOCAL * 128)

    def pass_gate(n):
        src = g_v.at[:, last_heads(b)] if n is None else g_t.at[n, :, last_heads(0)]
        n = b if n is None else n
        return remote(src, g_n.at[n], gns.at[0], gnr.at[0], (b, nxt))

    def pass_part(n):
        src = w_v.at[:, last_heads(b)] if n is None else w_t.at[n, :, last_heads(0)]
        n = b if n is None else n
        return remote(src, w_n.at[n], wns.at[0], wnr.at[0], (b, nxt))

    own_gate = pltpu.make_async_copy(g_v.at[:, cols(b)], g_t.at[b], oloc.at[0])
    own_gate.start()

    def values_here(g):
        xt = [xs[g, t] for t in range(chunk)]
        cur = res_v[:, lanes(g)]
        rate = ta[g]
        taps = []
        for t in range(chunk):
            taps.append(jnp.broadcast_to(jnp.sum(cur, axis=0, keepdims=True), (SUB, 128)))
            cur = cur * rate
            if t == 0:
                et[...] = cur
        skip = jnp.broadcast_to(skip_v[:, lanes(g)], (SUB, 128))
        y = []
        for t in range(chunk):
            acc = (skip + taps[0]) * xt[t]
            for k in range(1, t + 1):
                acc = acc + taps[k] * xt[t - k]
            y.append(acc)
        for m in range(modes):
            a = wide(ta, g, m)
            d = jnp.broadcast_to(et[pl.ds(m, 1), :], (SUB, 128)) * pm[g, m]
            for t in range(chunk):
                y[t] = y[t] + d
                if t + 1 < chunk:
                    d = d * a
        for t in range(chunk):
            xf[pl.ds(t, SUB, stride=chunk), :] = y[t]
        w_v[:, lanes(g)] = (g_v[:, lanes(g)].astype(F32) * xf[...]).astype(BF16)

    def values_step(n, carry):
        to = (b + 1 + n) % bins

        def one(j, inner):
            values_here(to * hg + j)
            return inner

        lax.fori_loop(0, hg, one, 0)

        @pl.when(to != b)
        def _():
            send_part(to)

        return carry

    with jax.named_scope("values"):
        lax.fori_loop(0, bins, values_step, 0)
    own_part = pltpu.make_async_copy(w_v.at[:, cols(b)], w_t.at[b], oloc.at[1])
    own_part.start()

    with jax.named_scope("near_states"):
        whole_of(e_r.at[pl.ds(0, near - 1)], l1s, l1r).wait_recv()
    step, leap = [], []
    for j in range(own):
        rate = lam_v[:, lanes(q * own + j)]
        step.append(jnp.exp(rate * (-1.0 * tokens)))
        leap.append(jnp.exp(rate * (-1.0 * tokens * near)))
        acc = jnp.zeros((modes, 128), F32)
        for n in range(near):
            pre[n, j] = acc
            acc = step[j] * acc + e_r[n, j].astype(F32)
        t_s[j] = acc.astype(STATE)

    def to_column(z):
        return remote(t_s, t_r.at[gz], l2s.at[0], l2r.at[0], at(gx, z))

    t_r[gz] = t_s[...]
    for z in (1, 2, 3):
        if z < far_z:

            @pl.when(gz == z)
            def _():
                for other in heard[z]:
                    if other < far_z:
                        to_column(other).start()
                if z != 2 and far_z == 4:
                    with jax.named_scope("second"):
                        pl.semaphore_wait(second_sem, 1)
                    to_column(4 - z).start()

    with jax.named_scope("peers"):
        pl.semaphore_wait(peer_sem, bins - 1)
    for i in range(bins):
        for r in range(parts):

            @pl.when(jnp.logical_not((i == b) & (b * parts + r == q)))
            def _():
                tell(home_sem, near_dev(b * parts + r, i))

    def gate_from(frm):
        return remote(g_v.at[:, cols(frm)], g_t.at[frm], gs.at[0], gr.at[0], (frm, c))

    def part_from(frm):
        return remote(w_v.at[:, cols(frm)], w_t.at[frm], ws.at[0], wr.at[0], (frm, c))

    def take_gates():
        own_gate.wait()
        with jax.named_scope("gates"):
            whole_of(g_t.at[pl.ds(0, bins - 1)], gs, gr).wait_recv()

    def take_parts():
        @pl.when(c + 1 < ctx)
        def _():
            pass_gate(None).start()
            for k in range(1, bins):
                pass_gate((b + k) % bins).start()
            pass_part(None).start()

        own_part.wait()
        with jax.named_scope("parts"):
            whole_of(w_t.at[pl.ds(0, bins - 1)], ws, wr).wait_recv()

        @pl.when(c + 1 < ctx)
        def _():
            for k in range(1, bins):
                pass_part((b + k) % bins).start()

    def send_weights(to):
        remote(p_v.at[pl.ds(to * hg, hg)], p_t.at[b], ps.at[0], pr.at[0], (to, c)).start()

    soon = gz < far_z - 1

    def take_weights():
        @pl.when(c > 0)
        def _():
            with jax.named_scope("keys"):
                key_send.wait_recv()
                id_send.wait_recv()

        @pl.when(c == 0)
        def _():
            k_n[...] = jnp.zeros_like(k_n)
            id_n[...] = jnp.zeros_like(id_n)

        t_idx = lax.broadcasted_iota(jnp.int32, (tokens, tokens), 0)
        u_idx = lax.broadcasted_iota(jnp.int32, (tokens, tokens), 1)
        lower = u_idx <= t_idx
        low[...] = lower.astype(F32).astype(BF16)
        upp[...] = (u_idx > t_idx).astype(F32).astype(BF16)
        id_row = jnp.broadcast_to(id_s[0:1, :].astype(F32), (tokens, tokens))
        id_col = id_row.T
        shut = jnp.where(c == 0, 65536.0, 0.0)
        id_before = jnp.broadcast_to(id_n[0:1, :].astype(F32), (tokens, tokens)) + shut
        id_key = jnp.where(lower, id_row, id_before)
        bias[...] = jnp.where(id_key == id_col, 0.0, -1e30)

        def weights_step(n, carry):
            to = (b + 1 + n) % bins
            for j in range(hg):
                h = to * hg + j
                query = q_v[:, lanes(h)]
                dn = (((1,), (1,)), ((), ()))
                s_own = lax.dot_general(query, k_v[:, lanes(h)], dn, preferred_element_type=F32)
                s_prev = lax.dot_general(query, k_n[:, lanes(h)], dn, preferred_element_type=F32)
                u_i = lax.broadcasted_iota(jnp.int32, (tokens, tokens), 1)
                t_i = lax.broadcasted_iota(jnp.int32, (tokens, tokens), 0)
                s = jnp.where(u_i <= t_i, s_own, s_prev) * HEAD_DIM ** (-0.5) + bias[...]
                e = jnp.exp(s - jnp.max(s, axis=1, keepdims=True))
                p_v[h] = (e * (1.0 / jnp.sum(e, axis=1, keepdims=True))).astype(BF16)

            @pl.when((to != b) & soon)
            def _():
                send_weights(to)

            return carry

        with jax.named_scope("weights"):
            lax.fori_loop(0, bins, weights_step, 0)
        own_weights = pltpu.make_async_copy(p_v.at[pl.ds(b * hg, hg)], p_t.at[b], oloc.at[2])
        own_weights.start()

    waits_long = (gz == 0) & (q == 0) & (c > 0)

    @pl.when(jnp.logical_not(waits_long))
    def _():
        take_weights()

    take_gates()

    @pl.when(gz == 0)
    def _():
        with jax.named_scope("nigh"):
            pl.semaphore_wait(nigh_sem, 2 if far_z == 4 else 1)
        to_column(1).start()
        if far_z == 4:
            to_column(3).start()
            with jax.named_scope("afar"):
                pl.semaphore_wait(afar_sem, 1)
            to_column(2).start()

    @pl.when(gz == 0)
    def _():
        take_parts()

    ramp = (row + 1).astype(F32)

    def table_step(j, carry):
        g = b * hg + j
        ta8[j] = jnp.exp(lam_v[:, lanes(g)] * (-1.0 * SUB))
        for m in range(modes):
            rate = jnp.broadcast_to(lam_v[pl.ds(m, 1), lanes(g)], (SUB, 128))
            weight = jnp.broadcast_to(res_v[pl.ds(m, 1), lanes(g)], (SUB, 128))
            gtab[j, m] = weight * jnp.exp(-rate * ramp)
        return carry

    lax.fori_loop(0, hg, table_step, 0)

    with jax.named_scope("totals"):
        whole_of(t_r.at[pl.ds(0, far_z - 1)], l2s, l2r).wait_recv()
    inside = []
    for j in range(own):
        whole_row, part_row = jnp.zeros((modes, 128), F32), jnp.zeros((modes, 128), F32)
        for z in range(far_z):
            total = t_r[z, j].astype(F32)
            whole_row = leap[j] * whole_row + total
            part_row = jnp.where(z < gz, leap[j] * part_row + total, part_row)
        inside.append(part_row)
        u_s[j] = whole_row.astype(STATE)

    def to_row(x):
        return remote(u_s, u_r.at[gx], l4s.at[x], l4r.at[gx], at(x, gz))

    for x in reversed(range(far_x)):

        @pl.when(x > gx)
        def _():
            to_row(x).start()

    def earlier(n, carry):
        remote(u_s, u_r.at[n], l4s.at[0], l4r.at[n], (b, c)).wait_recv()
        return tuple(
            row_leap[j] * carry[j] + u_r[n, j].astype(F32) for j in range(own)
        )

    row_leap = [jnp.exp(lam_v[:, lanes(q * own + j)] * (-1.0 * tokens * near * far_z)) for j in range(own)]
    @pl.when(waits_long)
    def _():
        take_weights()

    with jax.named_scope("rows"):
        outside = lax.fori_loop(
            0, gx, earlier, tuple(jnp.zeros((modes, 128), F32) for _ in range(own))
        )
    reach = gz.astype(F32) * (-1.0 * tokens * near)
    start = [
        inside[j] + jnp.exp(lam_v[:, lanes(q * own + j)] * reach) * outside[j] for j in range(own)
    ]
    for j in range(own):
        power = start[j]
        for n in range(near):
            c_s[n, j] = (pre[n, j] + power).astype(STATE)
            power = power * step[j]
    spot = pl.ds(lot * own, own)

    def to_home(n):
        return remote(c_s.at[n], c_r.at[b, spot], l3s.at[0], l3r.at[0], near_dev(n, home))

    def to_follower(n):
        some = c_s.at[n, pl.ds(own - LOCAL, LOCAL)]
        return remote(some, c_p.at[b], l3e.at[0], l3p.at[0], near_dev(n + 1, home))

    def at_home(n):
        return (home == b) & (q == n)

    def has_follower(n):
        return to_next_group if n == near - 1 else (lot == parts - 1) & jnp.logical_not(at_home(n + 1))

    with jax.named_scope("homes"):
        pl.semaphore_wait(home_sem, near - jnp.where(home == b, 1, 0))
    for n in range(near):

        @pl.when(jnp.logical_not(at_home(n)))
        def _():
            to_home(n).start()

        @pl.when(at_home(n))
        def _():
            c_r[b, spot] = c_s[n]

    for n in range(near):

        @pl.when(has_follower(n))
        def _():
            to_follower(n).start()

        if n + 1 < near:

            @pl.when((lot == parts - 1) & at_home(n + 1))
            def _():
                c_p[b] = c_s[n, own - LOCAL :]

    @pl.when(jnp.logical_not(soon))
    def _():
        for k in range(1, bins):
            send_weights((b + k) % bins)

    whole_of(e_r.at[pl.ds(0, near - 1)], l1s, l1r).wait_send()
    whole_of(t_r.at[pl.ds(0, far_z - 1)], l2s, l2r).wait_send()

    @pl.when(c + 1 < ctx)
    def _():
        key_send.wait_send()
        id_send.wait_send()

    whole_of(g_t.at[pl.ds(0, bins - 1)], gs, gr).wait_send()
    whole_of(bs_t.at[pl.ds(0, bins - 1)], bss, bsr).wait_send()

    @pl.when(gz > 0)
    def _():
        take_parts()


    @pl.when(home == b)
    def _():
        with jax.named_scope("states_in"):
            whole_of(c_s.at[pl.ds(0, near - 1)], l3s, l3r).wait_recv()

    @pl.when(home != b)
    def _():
        with jax.named_scope("states_in"):
            whole_of(c_s, l3s, l3r).wait_recv()

    def to_next(j):
        return remote(v_s.at[j], v_n.at[j], vs.at[j], vr.at[j], (b, nxt))

    def whole(j, bb, states_of, part, gate):
        ct[...] = states_of.astype(F32)
        acc = [jnp.zeros((SUB, 128), F32) for _ in range(tokens // SUB)]
        for m in range(modes):
            d = gtab[j, m] * jnp.broadcast_to(ct[pl.ds(m, 1), :], (SUB, 128))
            a = wide(ta8, j, m)
            for t in range(tokens // SUB):
                acc[t] = acc[t] + d
                if t + 1 < tokens // SUB:
                    d = d * a
        conv = jnp.concatenate(acc, axis=0)
        return (part.astype(F32) + gate.astype(F32) * conv).astype(BF16)

    def full(j):
        def one(bb, inner):
            v_s[j, bb] = whole(j, bb, c_r[bb, j], w_t[bb, :, lanes(j)], g_t[bb, :, lanes(j)])
            return inner

        lax.fori_loop(0, bins, one, 0)

    def full_step(j, carry):
        full(j)

        @pl.when(c + 1 < ctx)
        def _():
            to_next(j).start()

        return carry

    with jax.named_scope("full"):
        lax.fori_loop(0, hg - LOCAL, full_step, 0)

        def own_step(j, carry):
            full(j)
            return carry

        lax.fori_loop(hg - LOCAL, hg, own_step, 0)

    pltpu.make_async_copy(p_v.at[pl.ds(b * hg, hg)], p_t.at[b], oloc.at[2]).wait()
    with jax.named_scope("weights_in"):
        whole_of(p_t.at[pl.ds(0, bins - 1)], ps, pr).wait_recv()
        whole_of(bs_t.at[pl.ds(0, bins - 1)], bss, bsr).wait_recv()

    @pl.when(c == 0)
    def _():
        v_n[...] = jnp.zeros_like(v_n)

    def piece(j, to):
        return remote(
            o_s.at[j, to],
            out_h.at[0, :, lanes(b * hg + j)],
            os_.at[0],
            or_.at[0],
            (to, c),
        )

    def own_piece(j):
        return pltpu.make_async_copy(o_s.at[j, b], out_h.at[0, :, lanes(b * hg + j)], oloc.at[3 + j])

    def mix(j):
        for bb in range(bins):
            w = p_t[bb, j]
            o = jnp.dot(w * low[...], v_s[j, bb], preferred_element_type=F32)
            o = o + jnp.dot(w * upp[...], v_n[j, bb], preferred_element_type=F32)
            o_f[2 * bb] = o[:half]
            o_f[2 * bb + 1] = o[half:]

        def deal(n, inner):
            to = (b + jnp.where(n == 0, bins // 2, jnp.where(n <= bins // 2 - 1, n, n + 1))) % bins
            for s in range(2):
                pick = jnp.broadcast_to(bs_t[to, pl.ds(s, 1), :], (half, 128))
                got = o_f[0]
                for src in range(1, 2 * bins):
                    got = jnp.where(pick == src, o_f[src], got)
                o_s[j, to, pl.ds(s * half, half), :] = got.astype(BF16)

            @pl.when(to != b)
            def _():
                piece(j, to).start()

            return inner

        lax.fori_loop(0, bins, deal, 0)
        own_piece(j).start()

    @pl.when(c > 0)
    def _():
        with jax.named_scope("gates_before"):
            whole_of(g_n, gns, gnr).wait_recv()
        with jax.named_scope("parts_before"):
            whole_of(w_n, wns, wnr).wait_recv()
        self_follows = (q == b * parts + parts - 1) & (q > 0)

        @pl.when(self_follows)
        def _():
            with jax.named_scope("states_before"):
                whole_of(c_p.at[pl.ds(0, bins - 1)], l3e, l3p).wait_recv()

        @pl.when(jnp.logical_not(self_follows))
        def _():
            with jax.named_scope("states_before"):
                whole_of(c_p, l3e, l3p).wait_recv()

    def local_step(j, carry):
        @pl.when(c > 0)
        def _():
            def one(bb, inner):
                at_j = lanes(j - (hg - LOCAL))
                v_n[j, bb] = whole(
                    j, bb, c_p[bb, j - (hg - LOCAL)], w_n[bb, :, at_j], g_n[bb, :, at_j]
                )
                return inner

            lax.fori_loop(0, bins, one, 0)

        mix(j)
        return carry

    def halo_step(j, carry):
        @pl.when(c > 0)
        def _():
            with jax.named_scope("values_in"):
                to_next(j).wait_recv()

        mix(j)
        return carry

    with jax.named_scope("attention_last"):
        lax.fori_loop(hg - LOCAL, hg, local_step, 0)
    @pl.when(home == b)
    def _():
        whole_of(c_s.at[pl.ds(0, near - 1)], l3s, l3r).wait_send()

    @pl.when(home != b)
    def _():
        whole_of(c_s, l3s, l3r).wait_send()

    followers = near - 1 - jnp.where((home == b) & (q > 0), 1, 0) + jnp.where(to_next_group, 1, 0)
    for n in range(max(near - 2, 1), near + 1):

        @pl.when((lot == parts - 1) & (followers == n))
        def _():
            whole_of(c_s.at[pl.ds(0, n), pl.ds(0, LOCAL)], l3e, l3p).wait_send()

    for x in range(far_x):

        @pl.when(x > gx)
        def _():
            to_row(x).wait_send()

    whole_of(w_t.at[pl.ds(0, bins - 1)], ws, wr).wait_send()
    whole_of(p_t.at[pl.ds(0, bins - 1)], ps, pr).wait_send()

    with jax.named_scope("attention"):
        lax.fori_loop(0, hg - LOCAL, halo_step, 0)

    with jax.named_scope("last_sends"):

        @pl.when(c + 1 < ctx)
        def _():
            for j in range(hg - LOCAL):
                to_next(j).wait_send()
            whole_of(g_n, gns, gnr).wait_send()
            whole_of(w_n, wns, wnr).wait_send()

    for j in list(range(hg - LOCAL, hg)) + list(range(hg - LOCAL)):
        with jax.named_scope("out_own"):
            own_piece(j).wait()
    with jax.named_scope("out_send"):
        whole_of(o_s.at[:, pl.ds(0, bins - 1)], os_, or_).wait_send()
    with jax.named_scope("out_in"):
        others = out_h.at[0, pl.ds(0, tokens * (bins - 1) // bins)]
        whole_of(others, os_, or_).wait_recv()


def per_device(mesh_shape, x, gate, residues, rates, skip, queries, keys, ids, source):
    bins, ctx, near, groups, far_z, far_x = plan(mesh_shape)
    tokens, channels = x.shape[1:]
    modes = residues.shape[0]
    lg = channels // 128
    own = lg // near
    hg = lg // bins
    dims = (bins, ctx, near, groups, far_z, far_x, tokens, channels, modes)
    hbm = pl.BlockSpec(memory_space=pl.ANY)
    vmem = pltpu.VMEM
    dma = pltpu.SemaphoreType.DMA
    scratch = [
        vmem((tokens, channels), BF16),
        vmem((tokens, channels), BF16),
        vmem((modes, channels), F32),
        vmem((modes, channels), F32),
        vmem((1, channels), F32),
        vmem((tokens, channels), BF16),
        vmem((tokens, channels), BF16),
        vmem((1, tokens), jnp.int32),
        vmem((tokens, 128), F32),
        vmem((lg, tokens // SUB, SUB, 128), F32),
        vmem((lg, modes, SUB, 128), F32),
        vmem((lg, modes, 128), F32),
        vmem((lg, modes, 128), F32),
        vmem((lg, modes, 128), F32),
        vmem((lg, modes, 128), F32),
        vmem((modes, 128), F32),
        vmem((lg, modes, 128), STATE),
        vmem((near, own, modes, 128), STATE),
        vmem((near, own, modes, 128), F32),
        vmem((own, modes, 128), STATE),
        vmem((far_z, own, modes, 128), STATE),
        vmem((own, modes, 128), STATE),
        vmem((far_x, own, modes, 128), STATE),
        vmem((near, own, modes, 128), STATE),
        vmem((bins, hg, modes, 128), STATE),
        vmem((tokens, channels), BF16),
        vmem((lg, tokens, tokens), BF16),
        vmem((bins, tokens, hg * 128), BF16),
        vmem((bins, tokens, hg * 128), BF16),
        vmem((bins, hg, tokens, tokens), BF16),
        vmem((tokens, channels), BF16),
        vmem((SUB, 128), jnp.int32),
        vmem((SUB, 128), jnp.int32),
        vmem((SUB, 128), jnp.int32),
        vmem((bins, SUB, 128), jnp.int32),
        vmem((tokens, tokens), F32),
        vmem((tokens, tokens), BF16),
        vmem((tokens, tokens), BF16),
        vmem((hg, modes, SUB, 128), F32),
        vmem((hg, modes, 128), F32),
        vmem((modes, 128), F32),
        vmem((hg, bins, tokens, 128), BF16),
        vmem((hg, bins, tokens, 128), BF16),
        vmem((2 * bins, tokens // 2, 128), F32),
        vmem((hg, bins, tokens, 128), BF16),
        vmem((bins, tokens, LOCAL * 128), BF16),
        vmem((bins, tokens, LOCAL * 128), BF16),
        vmem((bins, LOCAL, modes, 128), STATE),
        dma((8,)),
        dma((1,)), dma((1,)),
        dma((1,)), dma((1,)),
        dma((far_x,)), dma((far_x,)),
        dma((1,)), dma((1,)),
        dma((1,)), dma((1,)),
        dma((1,)), dma((1,)),
        dma((1,)), dma((1,)),
        dma((1,)), dma((1,)),
        dma((1,)), dma((1,)),
        dma, dma,
        dma, dma,
        dma((hg,)), dma((hg,)),
        dma((1,)), dma((1,)),
        dma((1,)), dma((1,)),
        dma((1,)), dma((1,)),
        dma((3 + hg,)),
        dma((bins,)),
    ] + [pltpu.SemaphoreType.REGULAR] * 5
    return pl.pallas_call(
        functools.partial(kernel, dims),
        out_shape=jax.ShapeDtypeStruct((1, tokens, channels), BF16),
        in_specs=[hbm] * 8 + [pl.BlockSpec(memory_space=pltpu.SMEM)],
        out_specs=hbm,
        scratch_shapes=scratch,
        compiler_params=pltpu.CompilerParams(
            collective_id=0, has_side_effects=True, vmem_limit_bytes=56 * 1024 * 1024
        ),
        name="hybrid_pair",
    )(x, gate, residues, rates, skip.reshape(1, -1), queries, keys, ids, source)


def solution(mesh):
    rows = P("bins", "ctx", None)
    pairs = P("bins", "ctx")
    return jax.shard_map(
        functools.partial(per_device, dict(mesh.shape)),
        mesh=mesh,
        in_specs=(rows, rows, P(), P(), P(), rows, rows, pairs, pairs),
        out_specs=rows,
        check_vma=False,
    )
```

```python
import functools

import jax
import jax.numpy as jnp
from jax import lax
from jax.experimental import pallas as pl
from jax.experimental.pallas import tpu as pltpu
from jax.sharding import PartitionSpec as P

MESH = pl.DeviceIdType.MESH
HEAD_DIM = 128
SUB = 8
F32 = jnp.float32
BF16 = jnp.bfloat16
STATE = BF16
LOCAL = 1


def plan(mesh_shape):
    bins, ctx = mesh_shape["bins"], mesh_shape["ctx"]
    near = 8 if ctx >= 64 else 2
    groups = ctx // near
    far_z = 4 if groups >= 16 else 2
    return bins, ctx, near, groups, far_z, groups // far_z


def kernel(
    dims,
    x_h, g_h, res_h, lam_h, skip_h, q_h, k_h, ids_h, bs_s,
    out_h,
    x_v, g_v, res_v, lam_v, skip_v, q_v, k_v, ids_v,
    xf, xs, pm, ta, ta16, ta32, ta64, et, e_s, e_r, pre, t_s, t_r, u_s, u_r, c_s, c_r,
    w_v, p_v, w_t, g_t, p_t, k_n, id_s, id_n, bs_own, bs_t, bias, low, upp,
    gtab, ta8, ct, v_s, v_n, o_f, o_s, g_n, w_n, c_p,
    loc, l1s, l1r, l2s, l2r, l4s, l4r, l3s, l3r, l3e, l3p, gs, gr, ws, wr, ps, pr, bss, bsr,
    ks, kr, ids_, idr, vs, vr, gns, gnr, wns, wnr, os_, or_, oloc, xl, home_sem, peer_sem, second_sem, nigh_sem, afar_sem,
):
    bins, ctx, near, groups, far_z, far_x, tokens, channels, modes = dims
    lane_groups = channels // 128
    own = lane_groups // near
    hg = lane_groups // bins
    width = hg * 128
    parts = hg // own
    chunk = tokens // SUB
    half = tokens // 2

    b = lax.axis_index("bins")
    c = lax.axis_index("ctx")
    grp = c // near
    q = c % near
    gx, gz = grp // far_z, grp % far_z
    home, lot = q // parts, q % parts
    nxt = (c + 1) % ctx

    def remote(src, dst, ss, rs, dev):
        return pltpu.make_async_remote_copy(
            src_ref=src, dst_ref=dst, send_sem=ss, recv_sem=rs, device_id=dev, device_id_type=MESH
        )

    def whole_of(ref, ss, rs):
        return remote(ref, ref, ss.at[0], rs.at[0], (b, c))

    def lanes(index):
        return pl.ds(pl.multiple_of(index * 128, 128), 128)

    def cols(index):
        return pl.ds(pl.multiple_of(index * width, 128), width)

    def part_at(k):
        flip = near - 1 - k
        part, bit = 0, 1
        while bit < near:
            mine, other = (q // bit) % 2, (flip // bit) % 2
            part = part + bit * (mine + other - 2 * mine * other)
            bit *= 2
        return part

    def x_load(bin_):
        return pltpu.make_async_copy(x_h.at[0, :, cols(bin_)], x_v.at[:, cols(bin_)], xl.at[bin_])

    loads = [
        pltpu.make_async_copy(s, d, loc.at[n])
        for n, (s, d) in enumerate(
            [(lam_h, lam_v), (g_h.at[0], g_v), (k_h.at[0], k_v), (res_h, res_v), (skip_h, skip_v),
             (q_h.at[0], q_v), (ids_h, ids_v)]
        )
    ]
    loads[0].start()
    for k in range(0, near, parts):
        x_load(part_at(k) // parts).start()

    bar = pltpu.get_barrier_semaphore()

    def greet(dev):
        pl.semaphore_signal(bar, inc=1, device_id=dev, device_id_type=MESH)

    def at(x, z):
        return (b, (x * far_z + z) * near + q)

    def near_dev(n, bin_=b):
        return (bin_, grp * near + n)

    heard = {0: (), 1: (0, 2), 2: (0, 1, 3), 3: (0, 2)}
    row_devs = [at((gx + k) % far_x, gz) for k in range(1, far_x)]
    for z in range(far_z):
        ears = [other for other in range(far_z) if z in heard[other]]

        @pl.when(gz == z)
        def _():
            for other in ears:
                greet(at(gx, other))

    for dev in row_devs:
        greet(dev)
    for k in range(1, near):
        greet(near_dev((q + k) % near))
    count = (near - 1) + (bins - 1) + (far_x - 1)
    count = count + sum(
        jnp.where(gz == z, len([other for other in heard[z] if other < far_z]), 0) for z in range(far_z)
    )
    for k in range(1, bins):
        greet(((b + k) % bins, c))

    @pl.when(c > 0)
    def _():
        greet((b, c - 1))

    count = count + jnp.where(c + 1 < ctx, 1, 0)
    to_next_group = (lot == parts - 1) & (grp + 1 < groups)
    count = count + jnp.where(to_next_group, 1, 0)

    @pl.when((q == 0) & (grp > 0))
    def _():
        for i in range(bins):
            greet((i, (grp - 1) * near + b * parts + parts - 1))

    with jax.named_scope("rates_load"):
        loads[0].wait()
    loads[1].start()
    loads[2].start()
    row = lax.broadcasted_iota(jnp.int32, (SUB, 128), 0)
    m1 = (row >= 1).astype(F32)
    m2 = (row >= 2).astype(F32)
    m4 = (row >= 4).astype(F32)

    def wide(ref, g, m):
        return jnp.broadcast_to(ref[g, pl.ds(m, 1), :], (SUB, 128))

    def states(g):
        rate = lam_v[:, lanes(g)]
        ta[g] = jnp.exp(-rate)
        ta16[g] = jnp.exp(rate * (-1.0 * chunk))
        ta32[g] = jnp.exp(rate * (-2.0 * chunk))
        ta64[g] = jnp.exp(rate * (-4.0 * chunk))
        xf[...] = x_v[:, lanes(g)].astype(F32)
        xt = [xf[pl.ds(t, SUB, stride=chunk), :] for t in range(chunk)]
        for t in range(chunk):
            xs[g, t] = xt[t]
        for m in range(modes):
            a = wide(ta, g, m)
            e = xt[0]
            for t in range(1, chunk):
                e = e * a + xt[t]
            e = e + (wide(ta16, g, m) * m1) * pltpu.roll(e, 1, 0)
            e = e + (wide(ta32, g, m) * m2) * pltpu.roll(e, 2, 0)
            e = e + (wide(ta64, g, m) * m4) * pltpu.roll(e, 4, 0)
            pm[g, m] = pltpu.roll(e, 1, 0) * m1
            et[pl.ds(m, 1), :] = e[SUB - 1 :, :]
        e_s[g] = et[...].astype(STATE)

    def to_scan(part):
        return remote(
            e_s.at[pl.ds(part * own, own)], e_r.at[q], l1s.at[0], l1r.at[0], near_dev(part)
        )

    def send_states(k):
        @pl.when(part_at(k) != q)
        def _():
            to_scan(part_at(k)).start()

    def state_step(k, carry):
        @pl.when(k % parts == 0)
        def _():
            x_load(part_at(k) // parts).wait()

        for j in range(own):
            states(part_at(k) * own + j)
        return carry

    def state_send_step(k, carry):
        carry = state_step(k, carry)
        send_states(k)
        return carry

    lead = near
    with jax.named_scope("first_states"):
        lax.fori_loop(0, lead, state_step, 0)
    def tell(sem, dev):
        pl.semaphore_signal(sem, inc=1, device_id=dev, device_id_type=MESH)

    with jax.named_scope("barrier"):
        pl.semaphore_wait(bar, count)
    for z in (1, 2, 3):
        if z < far_z:

            @pl.when(gz == z)
            def _():
                tell(afar_sem if z == 2 else nigh_sem, at(gx, 0))
                if z == 2 and far_z == 4:
                    tell(second_sem, at(gx, 1))
                    tell(second_sem, at(gx, 3))


    for k in range(lead):
        send_states(k)
    for k in range(1, bins):
        tell(peer_sem, ((b + k) % bins, c))
    loads[2].wait()
    key_send = remote(k_v, k_n, ks, kr, (b, nxt))

    @pl.when(c + 1 < ctx)
    def _():
        key_send.start()

    loads[1].wait()

    def send_gates():
        for k in range(1, bins):
            to = (b + k) % bins
            remote(g_v.at[:, cols(to)], g_t.at[b], gs.at[0], gr.at[0], (to, c)).start()

    def send_part(to):
        remote(w_v.at[:, cols(to)], w_t.at[b], ws.at[0], wr.at[0], (to, c)).start()

    send_gates()

    for load in loads[3:]:
        load.start()
    with jax.named_scope("last_states"):
        lax.fori_loop(lead, near, state_send_step, 0)

    e_r[q] = e_s[pl.ds(q * own, own)]

    for load in loads[3:]:
        load.wait()
    id_s[...] = jnp.broadcast_to(ids_v[...], (SUB, 128))
    id_send = remote(id_s, id_n, ids_, idr, (b, nxt))

    @pl.when(c + 1 < ctx)
    def _():
        id_send.start()

    block_row = jnp.where(row == 0, bs_s[0, 0], bs_s[0, 1])
    bs_own[...] = block_row
    bs_t[b] = block_row
    for k in range(1, bins):
        to = (b + k) % bins
        remote(bs_own, bs_t.at[b], bss.at[0], bsr.at[0], (to, c)).start()
    def last_heads(bin_):
        return pl.ds(pl.multiple_of((bin_ * hg + hg - LOCAL) * 128, 128), LOCAL * 128)

    def pass_gate(n):
        src = g_v.at[:, last_heads(b)] if n is None else g_t.at[n, :, last_heads(0)]
        n = b if n is None else n
        return remote(src, g_n.at[n], gns.at[0], gnr.at[0], (b, nxt))

    def pass_part(n):
        src = w_v.at[:, last_heads(b)] if n is None else w_t.at[n, :, last_heads(0)]
        n = b if n is None else n
        return remote(src, w_n.at[n], wns.at[0], wnr.at[0], (b, nxt))

    own_gate = pltpu.make_async_copy(g_v.at[:, cols(b)], g_t.at[b], oloc.at[0])
    own_gate.start()

    def values_here(g):
        xt = [xs[g, t] for t in range(chunk)]
        cur = res_v[:, lanes(g)]
        rate = ta[g]
        taps = []
        for t in range(chunk):
            taps.append(jnp.broadcast_to(jnp.sum(cur, axis=0, keepdims=True), (SUB, 128)))
            cur = cur * rate
            if t == 0:
                et[...] = cur
        skip = jnp.broadcast_to(skip_v[:, lanes(g)], (SUB, 128))
        y = []
        for t in range(chunk):
            acc = (skip + taps[0]) * xt[t]
            for k in range(1, t + 1):
                acc = acc + taps[k] * xt[t - k]
            y.append(acc)
        for m in range(modes):
            a = wide(ta, g, m)
            d = jnp.broadcast_to(et[pl.ds(m, 1), :], (SUB, 128)) * pm[g, m]
            for t in range(chunk):
                y[t] = y[t] + d
                if t + 1 < chunk:
                    d = d * a
        for t in range(chunk):
            xf[pl.ds(t, SUB, stride=chunk), :] = y[t]
        w_v[:, lanes(g)] = (g_v[:, lanes(g)].astype(F32) * xf[...]).astype(BF16)

    def values_step(n, carry):
        to = (b + 1 + n) % bins

        def one(j, inner):
            values_here(to * hg + j)
            return inner

        lax.fori_loop(0, hg, one, 0)

        @pl.when(to != b)
        def _():
            send_part(to)

        return carry

    with jax.named_scope("values"):
        lax.fori_loop(0, bins, values_step, 0)
    own_part = pltpu.make_async_copy(w_v.at[:, cols(b)], w_t.at[b], oloc.at[1])
    own_part.start()

    with jax.named_scope("near_states"):
        whole_of(e_r.at[pl.ds(0, near - 1)], l1s, l1r).wait_recv()
    step, leap = [], []
    for j in range(own):
        rate = lam_v[:, lanes(q * own + j)]
        step.append(jnp.exp(rate * (-1.0 * tokens)))
        leap.append(jnp.exp(rate * (-1.0 * tokens * near)))
        acc = jnp.zeros((modes, 128), F32)
        for n in range(near):
            pre[n, j] = acc
            acc = step[j] * acc + e_r[n, j].astype(F32)
        t_s[j] = acc.astype(STATE)

    def to_column(z):
        return remote(t_s, t_r.at[gz], l2s.at[0], l2r.at[0], at(gx, z))

    t_r[gz] = t_s[...]
    for z in (1, 2, 3):
        if z < far_z:

            @pl.when(gz == z)
            def _():
                for other in heard[z]:
                    if other < far_z:
                        to_column(other).start()
                if z != 2 and far_z == 4:
                    with jax.named_scope("second"):
                        pl.semaphore_wait(second_sem, 1)
                    to_column(4 - z).start()

    with jax.named_scope("peers"):
        pl.semaphore_wait(peer_sem, bins - 1)
    for i in range(bins):
        for r in range(parts):

            @pl.when(jnp.logical_not((i == b) & (b * parts + r == q)))
            def _():
                tell(home_sem, near_dev(b * parts + r, i))

    def gate_from(frm):
        return remote(g_v.at[:, cols(frm)], g_t.at[frm], gs.at[0], gr.at[0], (frm, c))

    def part_from(frm):
        return remote(w_v.at[:, cols(frm)], w_t.at[frm], ws.at[0], wr.at[0], (frm, c))

    def take_gates():
        own_gate.wait()
        with jax.named_scope("gates"):
            whole_of(g_t.at[pl.ds(0, bins - 1)], gs, gr).wait_recv()

    def take_parts():
        @pl.when(c + 1 < ctx)
        def _():
            pass_gate(None).start()
            for k in range(1, bins):
                pass_gate((b + k) % bins).start()
            pass_part(None).start()

        own_part.wait()
        with jax.named_scope("parts"):
            whole_of(w_t.at[pl.ds(0, bins - 1)], ws, wr).wait_recv()

        @pl.when(c + 1 < ctx)
        def _():
            for k in range(1, bins):
                pass_part((b + k) % bins).start()

    def send_weights(to):
        remote(p_v.at[pl.ds(to * hg, hg)], p_t.at[b], ps.at[0], pr.at[0], (to, c)).start()

    soon = gz < far_z - 1

    def take_weights():
        @pl.when(c > 0)
        def _():
            with jax.named_scope("keys"):
                key_send.wait_recv()
                id_send.wait_recv()

        @pl.when(c == 0)
        def _():
            k_n[...] = jnp.zeros_like(k_n)
            id_n[...] = jnp.zeros_like(id_n)

        t_idx = lax.broadcasted_iota(jnp.int32, (tokens, tokens), 0)
        u_idx = lax.broadcasted_iota(jnp.int32, (tokens, tokens), 1)
        lower = u_idx <= t_idx
        low[...] = lower.astype(F32).astype(BF16)
        upp[...] = (u_idx > t_idx).astype(F32).astype(BF16)
        id_row = jnp.broadcast_to(id_s[0:1, :].astype(F32), (tokens, tokens))
        id_col = id_row.T
        shut = jnp.where(c == 0, 65536.0, 0.0)
        id_before = jnp.broadcast_to(id_n[0:1, :].astype(F32), (tokens, tokens)) + shut
        id_key = jnp.where(lower, id_row, id_before)
        bias[...] = jnp.where(id_key == id_col, 0.0, -1e30)

        def weights_step(n, carry):
            to = (b + 1 + n) % bins
            for j in range(hg):
                h = to * hg + j
                query = q_v[:, lanes(h)]
                dn = (((1,), (1,)), ((), ()))
                s_own = lax.dot_general(query, k_v[:, lanes(h)], dn, preferred_element_type=F32)
                s_prev = lax.dot_general(query, k_n[:, lanes(h)], dn, preferred_element_type=F32)
                u_i = lax.broadcasted_iota(jnp.int32, (tokens, tokens), 1)
                t_i = lax.broadcasted_iota(jnp.int32, (tokens, tokens), 0)
                s = jnp.where(u_i <= t_i, s_own, s_prev) * HEAD_DIM ** (-0.5) + bias[...]
                e = jnp.exp(s - jnp.max(s, axis=1, keepdims=True))
                p_v[h] = (e * (1.0 / jnp.sum(e, axis=1, keepdims=True))).astype(BF16)

            @pl.when((to != b) & soon)
            def _():
                send_weights(to)

            return carry

        with jax.named_scope("weights"):
            lax.fori_loop(0, bins, weights_step, 0)
        own_weights = pltpu.make_async_copy(p_v.at[pl.ds(b * hg, hg)], p_t.at[b], oloc.at[2])
        own_weights.start()

    waits_long = (gz == 0) & (q == 0) & (c > 0)

    @pl.when(jnp.logical_not(waits_long))
    def _():
        take_weights()

    take_gates()

    @pl.when(gz == 0)
    def _():
        with jax.named_scope("nigh"):
            pl.semaphore_wait(nigh_sem, 2 if far_z == 4 else 1)
        to_column(1).start()
        if far_z == 4:
            to_column(3).start()
            with jax.named_scope("afar"):
                pl.semaphore_wait(afar_sem, 1)
            to_column(2).start()

    @pl.when(gz == 0)
    def _():
        take_parts()

    ramp = (row + 1).astype(F32)

    def table_step(j, carry):
        g = b * hg + j
        ta8[j] = jnp.exp(lam_v[:, lanes(g)] * (-1.0 * SUB))
        for m in range(modes):
            rate = jnp.broadcast_to(lam_v[pl.ds(m, 1), lanes(g)], (SUB, 128))
            weight = jnp.broadcast_to(res_v[pl.ds(m, 1), lanes(g)], (SUB, 128))
            gtab[j, m] = weight * jnp.exp(-rate * ramp)
        return carry

    lax.fori_loop(0, hg, table_step, 0)

    with jax.named_scope("totals"):
        whole_of(t_r.at[pl.ds(0, far_z - 1)], l2s, l2r).wait_recv()
    inside = []
    for j in range(own):
        whole_row, part_row = jnp.zeros((modes, 128), F32), jnp.zeros((modes, 128), F32)
        for z in range(far_z):
            total = t_r[z, j].astype(F32)
            whole_row = leap[j] * whole_row + total
            part_row = jnp.where(z < gz, leap[j] * part_row + total, part_row)
        inside.append(part_row)
        u_s[j] = whole_row.astype(STATE)

    def to_row(x):
        return remote(u_s, u_r.at[gx], l4s.at[x], l4r.at[gx], at(x, gz))

    for x in reversed(range(far_x)):

        @pl.when(x > gx)
        def _():
            to_row(x).start()

    def earlier(n, carry):
        remote(u_s, u_r.at[n], l4s.at[0], l4r.at[n], (b, c)).wait_recv()
        return tuple(
            row_leap[j] * carry[j] + u_r[n, j].astype(F32) for j in range(own)
        )

    row_leap = [jnp.exp(lam_v[:, lanes(q * own + j)] * (-1.0 * tokens * near * far_z)) for j in range(own)]
    @pl.when(waits_long)
    def _():
        take_weights()

    with jax.named_scope("rows"):
        outside = lax.fori_loop(
            0, gx, earlier, tuple(jnp.zeros((modes, 128), F32) for _ in range(own))
        )
    reach = gz.astype(F32) * (-1.0 * tokens * near)
    start = [
        inside[j] + jnp.exp(lam_v[:, lanes(q * own + j)] * reach) * outside[j] for j in range(own)
    ]
    for j in range(own):
        power = start[j]
        for n in range(near):
            c_s[n, j] = (pre[n, j] + power).astype(STATE)
            power = power * step[j]
    spot = pl.ds(lot * own, own)

    def to_home(n):
        return remote(c_s.at[n], c_r.at[b, spot], l3s.at[0], l3r.at[0], near_dev(n, home))

    def to_follower(n):
        some = c_s.at[n, pl.ds(own - LOCAL, LOCAL)]
        return remote(some, c_p.at[b], l3e.at[0], l3p.at[0], near_dev(n + 1, home))

    def at_home(n):
        return (home == b) & (q == n)

    def has_follower(n):
        return to_next_group if n == near - 1 else (lot == parts - 1) & jnp.logical_not(at_home(n + 1))

    with jax.named_scope("homes"):
        pl.semaphore_wait(home_sem, near - jnp.where(home == b, 1, 0))
    for n in reversed(range(near)):

        @pl.when(jnp.logical_not(at_home(n)))
        def _():
            to_home(n).start()

        @pl.when(at_home(n))
        def _():
            c_r[b, spot] = c_s[n]

    for n in range(near):

        @pl.when(has_follower(n))
        def _():
            to_follower(n).start()

        if n + 1 < near:

            @pl.when((lot == parts - 1) & at_home(n + 1))
            def _():
                c_p[b] = c_s[n, own - LOCAL :]

    @pl.when(jnp.logical_not(soon))
    def _():
        for k in range(1, bins):
            send_weights((b + k) % bins)

    whole_of(e_r.at[pl.ds(0, near - 1)], l1s, l1r).wait_send()
    whole_of(t_r.at[pl.ds(0, far_z - 1)], l2s, l2r).wait_send()

    @pl.when(c + 1 < ctx)
    def _():
        key_send.wait_send()
        id_send.wait_send()

    whole_of(g_t.at[pl.ds(0, bins - 1)], gs, gr).wait_send()
    whole_of(bs_t.at[pl.ds(0, bins - 1)], bss, bsr).wait_send()

    @pl.when(gz > 0)
    def _():
        take_parts()


    @pl.when(home == b)
    def _():
        with jax.named_scope("states_in"):
            whole_of(c_s.at[pl.ds(0, near - 1)], l3s, l3r).wait_recv()

    @pl.when(home != b)
    def _():
        with jax.named_scope("states_in"):
            whole_of(c_s, l3s, l3r).wait_recv()

    def to_next(j):
        return remote(v_s.at[j], v_n.at[j], vs.at[j], vr.at[j], (b, nxt))

    def whole(j, bb, states_of, part, gate):
        ct[...] = states_of.astype(F32)
        acc = [jnp.zeros((SUB, 128), F32) for _ in range(tokens // SUB)]
        for m in range(modes):
            d = gtab[j, m] * jnp.broadcast_to(ct[pl.ds(m, 1), :], (SUB, 128))
            a = wide(ta8, j, m)
            for t in range(tokens // SUB):
                acc[t] = acc[t] + d
                if t + 1 < tokens // SUB:
                    d = d * a
        conv = jnp.concatenate(acc, axis=0)
        return (part.astype(F32) + gate.astype(F32) * conv).astype(BF16)

    def full(j):
        def one(bb, inner):
            v_s[j, bb] = whole(j, bb, c_r[bb, j], w_t[bb, :, lanes(j)], g_t[bb, :, lanes(j)])
            return inner

        lax.fori_loop(0, bins, one, 0)

    def full_step(j, carry):
        full(j)

        @pl.when(c + 1 < ctx)
        def _():
            to_next(j).start()

        return carry

    with jax.named_scope("full"):
        lax.fori_loop(0, hg - LOCAL, full_step, 0)

        def own_step(j, carry):
            full(j)
            return carry

        lax.fori_loop(hg - LOCAL, hg, own_step, 0)

    pltpu.make_async_copy(p_v.at[pl.ds(b * hg, hg)], p_t.at[b], oloc.at[2]).wait()
    with jax.named_scope("weights_in"):
        whole_of(p_t.at[pl.ds(0, bins - 1)], ps, pr).wait_recv()
        whole_of(bs_t.at[pl.ds(0, bins - 1)], bss, bsr).wait_recv()

    @pl.when(c == 0)
    def _():
        v_n[...] = jnp.zeros_like(v_n)

    def piece(j, to):
        return remote(
            o_s.at[j, to],
            out_h.at[0, :, lanes(b * hg + j)],
            os_.at[0],
            or_.at[0],
            (to, c),
        )

    def own_piece(j):
        return pltpu.make_async_copy(o_s.at[j, b], out_h.at[0, :, lanes(b * hg + j)], oloc.at[3 + j])

    def mix(j):
        for bb in range(bins):
            w = p_t[bb, j]
            o = jnp.dot(w * low[...], v_s[j, bb], preferred_element_type=F32)
            o = o + jnp.dot(w * upp[...], v_n[j, bb], preferred_element_type=F32)
            o_f[2 * bb] = o[:half]
            o_f[2 * bb + 1] = o[half:]

        def deal(n, inner):
            to = (b + jnp.where(n == 0, bins // 2, jnp.where(n <= bins // 2 - 1, n, n + 1))) % bins
            for s in range(2):
                pick = jnp.broadcast_to(bs_t[to, pl.ds(s, 1), :], (half, 128))
                got = o_f[0]
                for src in range(1, 2 * bins):
                    got = jnp.where(pick == src, o_f[src], got)
                o_s[j, to, pl.ds(s * half, half), :] = got.astype(BF16)

            @pl.when(to != b)
            def _():
                piece(j, to).start()

            return inner

        lax.fori_loop(0, bins, deal, 0)
        own_piece(j).start()

    @pl.when(c > 0)
    def _():
        with jax.named_scope("gates_before"):
            whole_of(g_n, gns, gnr).wait_recv()
        with jax.named_scope("parts_before"):
            whole_of(w_n, wns, wnr).wait_recv()
        self_follows = (q == b * parts + parts - 1) & (q > 0)

        @pl.when(self_follows)
        def _():
            with jax.named_scope("states_before"):
                whole_of(c_p.at[pl.ds(0, bins - 1)], l3e, l3p).wait_recv()

        @pl.when(jnp.logical_not(self_follows))
        def _():
            with jax.named_scope("states_before"):
                whole_of(c_p, l3e, l3p).wait_recv()

    def local_step(j, carry):
        @pl.when(c > 0)
        def _():
            def one(bb, inner):
                at_j = lanes(j - (hg - LOCAL))
                v_n[j, bb] = whole(
                    j, bb, c_p[bb, j - (hg - LOCAL)], w_n[bb, :, at_j], g_n[bb, :, at_j]
                )
                return inner

            lax.fori_loop(0, bins, one, 0)

        mix(j)
        return carry

    def halo_step(j, carry):
        @pl.when(c > 0)
        def _():
            with jax.named_scope("values_in"):
                to_next(j).wait_recv()

        mix(j)
        return carry

    with jax.named_scope("attention_last"):
        lax.fori_loop(hg - LOCAL, hg, local_step, 0)
    @pl.when(home == b)
    def _():
        whole_of(c_s.at[pl.ds(0, near - 1)], l3s, l3r).wait_send()

    @pl.when(home != b)
    def _():
        whole_of(c_s, l3s, l3r).wait_send()

    followers = near - 1 - jnp.where((home == b) & (q > 0), 1, 0) + jnp.where(to_next_group, 1, 0)
    for n in range(max(near - 2, 1), near + 1):

        @pl.when((lot == parts - 1) & (followers == n))
        def _():
            whole_of(c_s.at[pl.ds(0, n), pl.ds(0, LOCAL)], l3e, l3p).wait_send()

    for x in range(far_x):

        @pl.when(x > gx)
        def _():
            to_row(x).wait_send()

    whole_of(w_t.at[pl.ds(0, bins - 1)], ws, wr).wait_send()
    whole_of(p_t.at[pl.ds(0, bins - 1)], ps, pr).wait_send()

    with jax.named_scope("attention"):
        lax.fori_loop(0, hg - LOCAL, halo_step, 0)

    with jax.named_scope("last_sends"):

        @pl.when(c + 1 < ctx)
        def _():
            for j in range(hg - LOCAL):
                to_next(j).wait_send()
            whole_of(g_n, gns, gnr).wait_send()
            whole_of(w_n, wns, wnr).wait_send()

    for j in list(range(hg - LOCAL, hg)) + list(range(hg - LOCAL)):
        with jax.named_scope("out_own"):
            own_piece(j).wait()
    with jax.named_scope("out_send"):
        whole_of(o_s.at[:, pl.ds(0, bins - 1)], os_, or_).wait_send()
    with jax.named_scope("out_in"):
        others = out_h.at[0, pl.ds(0, tokens * (bins - 1) // bins)]
        whole_of(others, os_, or_).wait_recv()


def per_device(mesh_shape, x, gate, residues, rates, skip, queries, keys, ids, source):
    bins, ctx, near, groups, far_z, far_x = plan(mesh_shape)
    tokens, channels = x.shape[1:]
    modes = residues.shape[0]
    lg = channels // 128
    own = lg // near
    hg = lg // bins
    dims = (bins, ctx, near, groups, far_z, far_x, tokens, channels, modes)
    hbm = pl.BlockSpec(memory_space=pl.ANY)
    vmem = pltpu.VMEM
    dma = pltpu.SemaphoreType.DMA
    scratch = [
        vmem((tokens, channels), BF16),
        vmem((tokens, channels), BF16),
        vmem((modes, channels), F32),
        vmem((modes, channels), F32),
        vmem((1, channels), F32),
        vmem((tokens, channels), BF16),
        vmem((tokens, channels), BF16),
        vmem((1, tokens), jnp.int32),
        vmem((tokens, 128), F32),
        vmem((lg, tokens // SUB, SUB, 128), F32),
        vmem((lg, modes, SUB, 128), F32),
        vmem((lg, modes, 128), F32),
        vmem((lg, modes, 128), F32),
        vmem((lg, modes, 128), F32),
        vmem((lg, modes, 128), F32),
        vmem((modes, 128), F32),
        vmem((lg, modes, 128), STATE),
        vmem((near, own, modes, 128), STATE),
        vmem((near, own, modes, 128), F32),
        vmem((own, modes, 128), STATE),
        vmem((far_z, own, modes, 128), STATE),
        vmem((own, modes, 128), STATE),
        vmem((far_x, own, modes, 128), STATE),
        vmem((near, own, modes, 128), STATE),
        vmem((bins, hg, modes, 128), STATE),
        vmem((tokens, channels), BF16),
        vmem((lg, tokens, tokens), BF16),
        vmem((bins, tokens, hg * 128), BF16),
        vmem((bins, tokens, hg * 128), BF16),
        vmem((bins, hg, tokens, tokens), BF16),
        vmem((tokens, channels), BF16),
        vmem((SUB, 128), jnp.int32),
        vmem((SUB, 128), jnp.int32),
        vmem((SUB, 128), jnp.int32),
        vmem((bins, SUB, 128), jnp.int32),
        vmem((tokens, tokens), F32),
        vmem((tokens, tokens), BF16),
        vmem((tokens, tokens), BF16),
        vmem((hg, modes, SUB, 128), F32),
        vmem((hg, modes, 128), F32),
        vmem((modes, 128), F32),
        vmem((hg, bins, tokens, 128), BF16),
        vmem((hg, bins, tokens, 128), BF16),
        vmem((2 * bins, tokens // 2, 128), F32),
        vmem((hg, bins, tokens, 128), BF16),
        vmem((bins, tokens, LOCAL * 128), BF16),
        vmem((bins, tokens, LOCAL * 128), BF16),
        vmem((bins, LOCAL, modes, 128), STATE),
        dma((8,)),
        dma((1,)), dma((1,)),
        dma((1,)), dma((1,)),
        dma((far_x,)), dma((far_x,)),
        dma((1,)), dma((1,)),
        dma((1,)), dma((1,)),
        dma((1,)), dma((1,)),
        dma((1,)), dma((1,)),
        dma((1,)), dma((1,)),
        dma((1,)), dma((1,)),
        dma, dma,
        dma, dma,
        dma((hg,)), dma((hg,)),
        dma((1,)), dma((1,)),
        dma((1,)), dma((1,)),
        dma((1,)), dma((1,)),
        dma((3 + hg,)),
        dma((bins,)),
    ] + [pltpu.SemaphoreType.REGULAR] * 5
    return pl.pallas_call(
        functools.partial(kernel, dims),
        out_shape=jax.ShapeDtypeStruct((1, tokens, channels), BF16),
        in_specs=[hbm] * 8 + [pl.BlockSpec(memory_space=pltpu.SMEM)],
        out_specs=hbm,
        scratch_shapes=scratch,
        compiler_params=pltpu.CompilerParams(
            collective_id=0, has_side_effects=True, vmem_limit_bytes=56 * 1024 * 1024
        ),
        name="hybrid_pair",
    )(x, gate, residues, rates, skip.reshape(1, -1), queries, keys, ids, source)


def solution(mesh):
    rows = P("bins", "ctx", None)
    pairs = P("bins", "ctx")
    return jax.shard_map(
        functools.partial(per_device, dict(mesh.shape)),
        mesh=mesh,
        in_specs=(rows, rows, P(), P(), P(), rows, rows, pairs, pairs),
        out_specs=rows,
        check_vma=False,
    )
```
